128 devices in a mesh: gz: 32 (over y, x, core), gy: 4 (over z).
Axes of the slice: x: 4, y: 4, z: 4, core: 2. Of those that a mesh axis runs over, the one named last changes fastest.
Arguments:
- iterate: float32 [512, 256, 128], P('gz', 'gy'), may hold values from -13 to 13
- source: float32 [512, 256, 128], P('gz', 'gy'), may hold values from -27 to 27
- region: int32 [512, 256, 128], P('gz', 'gy'), may hold values from 0 to 2, as said below
- fixed_mask: int32 [512, 256, 128], P('gz', 'gy'), may hold values from 0 to 1, as said below
Outputs:
- correction: float32 [512, 256, 128], P('gz', 'gy')
- lin_residual: float32 [512, 256, 128], P('gz', 'gy')
- residual_rms: float32 [], replicated
The draws below stay inside these ranges and needn't reach their ends.
Inputs may be any that keep to these rules, and one draw needn't show every extreme that they name: `region`: the same at every z. `fixed_mask`: the same at every z.
All inputs are finite; a program needn't handle non-finite values.
Results may differ from the reference program's by a relative error of at most 0.007.
Values sent between devices are 32-bit elements; how exact they have to be, the bound alone decides.
No kernel may reach another device: no remote copies, remote signals or barrier semaphores. Data moves between devices by JAX's collectives and lax.ppermute only.
A program may use at most 64 MiB of HBM per device.

```python
import jax
import jax.numpy as jnp
from jax import lax

NZ = 512
NX = 128
SWEEPS = 4
NY = 256


def ramped(key, scale):
    key_a, key_b = jax.random.split(key)
    shape = (NZ, NY, NX)
    zpos = jnp.arange(NZ, dtype=jnp.int32).astype(jnp.float32)[:, None, None] / (NZ - 1)
    ramp = jnp.exp(jnp.log(3.0) * zpos)
    rough = jnp.exp(jax.random.uniform(key_b, shape, jnp.float32, -0.69, 0.69))
    base = jax.random.truncated_normal(key_a, -4.0, 4.0, shape, jnp.float32)
    return (scale * base * rough * ramp).astype(jnp.float32)


def motor_section(key):
    keys = jax.random.split(key, 5)
    rotor_radius = jax.random.randint(keys[0], (), 300, 401, dtype=jnp.int32)
    gap_width = jax.random.randint(keys[1], (), 30, 61, dtype=jnp.int32)
    outer_radius = jax.random.randint(keys[2], (), 820, 931, dtype=jnp.int32)
    shift_x = jax.random.randint(keys[3], (), -(NX // 16), NX // 16 + 1, dtype=jnp.int32)
    slot_phase = jax.random.randint(keys[4], (), 0, 8, dtype=jnp.int32)
    rows = jnp.arange(NY, dtype=jnp.int32)[:, None]
    cols = jnp.arange(NX, dtype=jnp.int32)[None, :]
    along_y = (2000 * rows - 1000 * NY) // NY
    along_x = (2000 * (cols - shift_x) - 1000 * NX) // NX
    radius_sq = along_y * along_y + along_x * along_x
    slot_wide = max(NX // 32, 1)
    slot_tall = max(NY // 16, 1)
    in_slot = ((cols + slot_phase) // slot_wide + rows // slot_tall) % 2 == 0
    stator_inner = rotor_radius + gap_width
    bars = (radius_sq >= (rotor_radius - 60) * (rotor_radius - 60)) & in_slot
    windings = (radius_sq < (stator_inner + 150) * (stator_inner + 150)) & in_slot
    outside = jnp.where(radius_sq < outer_radius * outer_radius, 2, 0)
    stator = jnp.where(windings, 1, outside)
    airgap = jnp.where(radius_sq < stator_inner * stator_inner, 0, stator)
    rotor = jnp.where(bars, 1, 2)
    section = jnp.where(radius_sq < rotor_radius * rotor_radius, rotor, airgap)
    boundary = jnp.where(radius_sq >= outer_radius * outer_radius, 1, 0)
    return (section.astype(jnp.int32), boundary.astype(jnp.int32))


def draw_iterate(key, part):
    key = jax.random.fold_in(key, 11)
    return ramped(key, 0.5)


def draw_source(key, part):
    key = jax.random.fold_in(key, 23)
    return ramped(key, 1.0)


def draw_region(key, part):
    section, boundary = motor_section(key)
    return jnp.broadcast_to(section[None, :, :], (NZ, NY, NX)).astype(jnp.int32)


def draw_fixed_mask(key, part):
    section, boundary = motor_section(key)
    return jnp.broadcast_to(boundary[None, :, :], (NZ, NY, NX)).astype(jnp.int32)


def setup_inputs(seed: int = 0) -> dict:
    streams_of = jax.random.split(jax.random.key(seed), 5)
    return {
        "iterate": draw_iterate(jax.random.fold_in(streams_of[4], 71), 0),
        "source": draw_source(jax.random.fold_in(streams_of[4], 71), 0),
        "region": draw_region(jax.random.fold_in(streams_of[4], 71), 0),
        "fixed_mask": draw_fixed_mask(jax.random.fold_in(streams_of[4], 71), 0),
    }


def dst_table(count):
    index = jnp.arange(count, dtype=jnp.int32)
    phase = (index[:, None] + 1) * (index[None, :] + 1) % (2 * (count + 1))
    return jnp.sqrt(2.0 / (count + 1)) * jnp.sin(jnp.pi * phase.astype(jnp.float32) / (count + 1))

def eigen_values(count):
    index = jnp.arange(count, dtype=jnp.int32).astype(jnp.float32)
    return 2.0 - 2.0 * jnp.cos(jnp.pi * (index + 1.0) / (count + 1))

def reluct(bsq, region):
    iron = 0.05 + bsq * bsq / (bsq * bsq + 9.0)
    return jnp.where(region == 2, iron, jnp.float32(1.0))

def face_terms(padded):
    center = padded[1:-1, 1:-1, 1:-1]
    return (0.5 * (center + padded[2:, 1:-1, 1:-1]), 0.5 * (center + padded[:-2, 1:-1, 1:-1]), 0.5 * (center + padded[1:-1, 2:, 1:-1]), 0.5 * (center + padded[1:-1, :-2, 1:-1]), 0.5 * (center + padded[1:-1, 1:-1, 2:]), 0.5 * (center + padded[1:-1, 1:-1, :-2]))

def stencil(field, padded, terms):
    near = (padded[2:, 1:-1, 1:-1], padded[:-2, 1:-1, 1:-1], padded[1:-1, 2:, 1:-1], padded[1:-1, :-2, 1:-1], padded[1:-1, 1:-1, 2:], padded[1:-1, 1:-1, :-2])
    total = jnp.zeros_like(field)
    for coef, other in zip(terms, near):
        total = total + coef * (field - other)
    return total

def smooth(vhat, lam, nbpad):
    center = nbpad[1:-1, 1:-1]
    cyp = 0.5 * (center + nbpad[2:, 1:-1])
    cym = 0.5 * (center + nbpad[:-2, 1:-1])
    cxp = 0.5 * (center + nbpad[1:-1, 2:])
    cxm = 0.5 * (center + nbpad[1:-1, :-2])
    diag = cyp + cym + cxp + cxm + lam[:, None, None] * center
    smoothed = jnp.zeros_like(vhat)
    for sweep in range(SWEEPS):
        wpad = jnp.pad(smoothed, ((0, 0), (1, 1), (1, 1)))
        near = cyp * wpad[:, 2:, 1:-1] + cym * wpad[:, :-2, 1:-1] + cxp * wpad[:, 1:-1, 2:] + cxm * wpad[:, 1:-1, :-2]
        smoothed = smoothed + 0.6 * (vhat - (diag * smoothed - near)) / diag
    return smoothed

def reference(iterate, source, region, fixed_mask):
    upad = jnp.pad(iterate, 1)
    bsq = (upad[2:, 1:-1, 1:-1] - iterate) ** 2 + (upad[1:-1, 2:, 1:-1] - iterate) ** 2 + (upad[1:-1, 1:-1, 2:] - iterate) ** 2
    nu = reluct(bsq, region)
    terms = face_terms(jnp.pad(nu, 1, constant_values=1.0))
    applied = stencil(iterate, upad, terms)
    resid = -jnp.where(fixed_mask == 1, iterate, applied - source * (region == 1).astype(jnp.float32))
    beta = jnp.sqrt(jnp.sum(resid * resid) + 1e-06)
    count = iterate.shape[0] * iterate.shape[1] * iterate.shape[2]
    residual_rms = beta / jnp.sqrt(jnp.float32(count))
    vector = resid / beta
    table = dst_table(iterate.shape[0])
    lam = eigen_values(iterate.shape[0])
    vhat = jnp.einsum('kj,jyx->kyx', table, vector, precision=lax.Precision.HIGHEST)
    nubar = lax.optimization_barrier(jnp.sum(nu, axis=0)) / iterate.shape[0]
    smoothed = smooth(vhat, lam, jnp.pad(nubar, 1, constant_values=1.0))
    zdir = jnp.einsum('kj,jyx->kyx', table, smoothed, precision=lax.Precision.HIGHEST)
    image = stencil(zdir, jnp.pad(zdir, 1), terms)
    image = jnp.where(fixed_mask == 1, zdir, image)
    h_one = jnp.sum(vector * image)
    ortho = image - h_one * vector
    h_two = jnp.sqrt(jnp.sum(ortho * ortho))
    gamma = beta * h_one / (h_one * h_one + h_two * h_two + 1e-06)
    return (gamma * zdir, resid - gamma * image, residual_rms)
```

```python
import jax
import jax.numpy as jnp
from jax import lax
from jax.sharding import PartitionSpec as P

SWEEPS = 4


def with_halo(array, sides, width):
    for axis, dim in sides:
        devices, length = (lax.axis_size(axis), array.shape[dim])
        up = [(i, (i + 1) % devices) for i in range(devices - 1)]
        down = [(j, i) for i, j in up]
        last = lax.slice_in_dim(array, length - width, length, axis=dim)
        first = lax.slice_in_dim(array, 0, width, axis=dim)
        before = lax.ppermute(last, axis, up)
        after = lax.ppermute(first, axis, down)
        array = jnp.concatenate([before, array, after], axis=dim)
    return array


def dst_table(count):
    index = jnp.arange(count, dtype=jnp.int32)
    phase = (index[:, None] + 1) * (index[None, :] + 1) % (2 * (count + 1))
    return jnp.sqrt(2.0 / (count + 1)) * jnp.sin(jnp.pi * phase.astype(jnp.float32) / (count + 1))


def eigen_values(index, count):
    return 2.0 - 2.0 * jnp.cos(jnp.pi * (index.astype(jnp.float32) + 1.0) / (count + 1))


def reluct(bsq, region):
    iron = 0.05 + bsq * bsq / (bsq * bsq + 9.0)
    return jnp.where(region == 2, iron, jnp.float32(1.0))


def slab_rimmed(field):
    padded = with_halo(field, (("gz", 0), ("gy", 1)), 1)
    return jnp.pad(padded, ((0, 0), (0, 0), (1, 1)))


def face_terms(padded):
    center = padded[1:-1, 1:-1, 1:-1]
    return (
        0.5 * (center + padded[2:, 1:-1, 1:-1]),
        0.5 * (center + padded[:-2, 1:-1, 1:-1]),
        0.5 * (center + padded[1:-1, 2:, 1:-1]),
        0.5 * (center + padded[1:-1, :-2, 1:-1]),
        0.5 * (center + padded[1:-1, 1:-1, 2:]),
        0.5 * (center + padded[1:-1, 1:-1, :-2]),
    )


def stencil(field, padded, terms):
    near = (
        padded[2:, 1:-1, 1:-1],
        padded[:-2, 1:-1, 1:-1],
        padded[1:-1, 2:, 1:-1],
        padded[1:-1, :-2, 1:-1],
        padded[1:-1, 1:-1, 2:],
        padded[1:-1, 1:-1, :-2],
    )
    total = jnp.zeros_like(field)
    for coef, other in zip(terms, near):
        total = total + coef * (field - other)
    return total


def smooth(vhat, lam, nbpad, rim_fn):
    center = nbpad[1:-1, 1:-1]
    cyp = 0.5 * (center + nbpad[2:, 1:-1])
    cym = 0.5 * (center + nbpad[:-2, 1:-1])
    cxp = 0.5 * (center + nbpad[1:-1, 2:])
    cxm = 0.5 * (center + nbpad[1:-1, :-2])
    diag = cyp + cym + cxp + cxm + lam[:, None, None] * center
    smoothed = jnp.zeros_like(vhat)
    for sweep in range(SWEEPS):
        wpad = rim_fn(smoothed)
        near = (
            cyp * wpad[:, 2:, 1:-1]
            + cym * wpad[:, :-2, 1:-1]
            + cxp * wpad[:, 1:-1, 2:]
            + cxm * wpad[:, 1:-1, :-2]
        )
        smoothed = smoothed + 0.6 * (vhat - (diag * smoothed - near)) / diag
    return smoothed


def mode_rimmed(field):
    padded = with_halo(field, (("gy", 1),), 1)
    return jnp.pad(padded, ((0, 0), (0, 0), (1, 1)))


def precondition(vector, column, table):
    zcells = vector.shape[0]
    groups = lax.axis_size("gz")
    order = zcells * groups
    group = lax.axis_index("gz")

    def transform(lines):
        return jnp.einsum("kj,jyx->kyx", table, lines, precision=lax.Precision.HIGHEST)

    def to_lines(field):
        return lax.all_to_all(field, "gz", split_axis=2, concat_axis=0, tiled=True)

    def to_slabs(lines):
        return lax.all_to_all(lines, "gz", split_axis=0, concat_axis=2, tiled=True)

    rows, part = vector.shape[1], vector.shape[2] // groups
    lines = to_lines(jnp.concatenate([vector, column[None]], axis=0))
    lines = lines.reshape(groups, zcells + 1, rows, part)
    mean = jnp.sum(lines[:, zcells], axis=0) / order
    vhat = transform(lines[:, :zcells].reshape(order, rows, part))
    packed = jnp.concatenate(
        [vhat.reshape(groups, zcells, rows, part), jnp.broadcast_to(mean, (groups, 1, rows, part))],
        axis=1,
    )
    modes = to_slabs(packed.reshape(groups * (zcells + 1), rows, part))
    nbpad = with_halo(modes[zcells] - 1.0, (("gy", 0),), 1) + 1.0
    nbpad = jnp.pad(nbpad, ((0, 0), (1, 1)), constant_values=1.0)
    index = group * zcells + jnp.arange(zcells, dtype=jnp.int32)
    smoothed = smooth(modes[:zcells], eigen_values(index, order), nbpad, mode_rimmed)
    return to_slabs(transform(to_lines(smoothed)))


def sum_all(values):
    devices = lax.axis_size("gz") * lax.axis_size("gy")
    packed = jnp.zeros((1, 128), jnp.float32)
    for place, value in enumerate(values):
        packed = packed.at[0, place].set(value)
    sent = jnp.broadcast_to(packed[None], (devices, 1, 128))
    got = lax.all_to_all(sent, ("gz", "gy"), split_axis=0, concat_axis=0, tiled=True)
    return jnp.sum(got, axis=(0, 1))


def shards(iterate, source, region, fixed_mask):
    zcells = iterate.shape[0]
    order = zcells * lax.axis_size("gz")
    upad = slab_rimmed(iterate)
    bsq = (
        (upad[2:, 1:-1, 1:-1] - iterate) ** 2
        + (upad[1:-1, 2:, 1:-1] - iterate) ** 2
        + (upad[1:-1, 1:-1, 2:] - iterate) ** 2
    )
    nu = reluct(bsq, region)
    nu_pad = with_halo(nu - 1.0, (("gz", 0), ("gy", 1)), 1) + 1.0
    nu_pad = jnp.pad(nu_pad, ((0, 0), (0, 0), (1, 1)), constant_values=1.0)
    terms = face_terms(nu_pad)
    applied = stencil(iterate, upad, terms)
    resid = -jnp.where(
        fixed_mask == 1, iterate, applied - source * (region == 1).astype(jnp.float32)
    )
    column = jnp.sum(nu, axis=0)
    table = dst_table(order)
    count = order * iterate.shape[1] * lax.axis_size("gy") * iterate.shape[2]
    zdir = precondition(resid, column, table)
    image = jnp.where(fixed_mask == 1, zdir, stencil(zdir, slab_rimmed(zdir), terms))
    sums = sum_all((jnp.sum(resid * resid), jnp.sum(resid * image), jnp.sum(image * image)))
    beta_sq = sums[0] + 1e-06
    beta = jnp.sqrt(beta_sq)
    h_one = sums[1] / beta_sq
    denom = sums[2] / beta_sq - h_one * h_one * (1e-06 / beta_sq) + 1e-06
    gamma = h_one / denom
    residual_rms = beta / jnp.sqrt(jnp.float32(count))
    return (gamma * zdir, resid - gamma * image, residual_rms)


def solution(mesh):
    placed = (P("gz", "gy", None), P("gz", "gy", None), P("gz", "gy", None), P("gz", "gy", None))
    return jax.shard_map(
        shards,
        mesh=mesh,
        in_specs=placed,
        out_specs=(P("gz", "gy", None), P("gz", "gy", None), P()),
        check_vma=False,
    )
```

```python
import functools

import jax
import jax.numpy as jnp
import ml_dtypes
import numpy as np
from jax import lax
from jax.experimental import pallas as pl
from jax.experimental.pallas import tpu as pltpu
from jax.sharding import PartitionSpec as P

F32 = jnp.float32
BF16 = jnp.bfloat16
NZ, NY, NX = 512, 256, 128
GZ, GY = 32, 4
ZC, YC = NZ // GZ, NY // GY
FR = YC + 16
WR, WC, RING = 23, 22, 3
LANES = 512
YP, XP = 4, 8
ROW0 = (0, 17, 33, 49)
VMEM_LIMIT = 40 * 1024 * 1024


def tables():
    index = np.arange(NZ, dtype=np.int64)
    phase = (index[:, None] + 1) * (index[None, :] + 1) % (2 * (NZ + 1))
    table = np.sqrt(2.0 / (NZ + 1)) * np.sin(np.pi * phase / (NZ + 1))
    table = table.astype(np.float32)
    high = table.astype(ml_dtypes.bfloat16)
    low = (table - high.astype(np.float32)).astype(ml_dtypes.bfloat16)
    lam = 2.0 - 2.0 * np.cos(np.pi * (index + 1.0) / (NZ + 1))
    lam = np.broadcast_to(lam.astype(np.float32)[:, None], (NZ, 128))
    return high, low, np.ascontiguousarray(lam)


def lane_iota(shape):
    return lax.broadcasted_iota(jnp.int32, shape, len(shape) - 1)


def roll(value, shift, axis):
    return pltpu.roll(value, shift % value.shape[axis], axis)


def halo_pack(first_it, last_it, zlo, zhi, first_src, last_src, first_reg, last_reg,
              first_msk, last_msk, down, up):
    for out, it, src, reg, msk, rows, low in (
        (down, first_it, first_src, first_reg, first_msk, 0, 0),
        (up, last_it, last_src, last_reg, last_msk, YC - 8, 4),
    ):
        out[0] = zlo[0, rows:rows + 8, :]
        out[1:17] = it[...]
        out[17] = zhi[0, rows:rows + 8, :]
        out[18] = zhi[1, rows:rows + 8, :]
        for pair in range(8):
            out[19 + pair, 0:4] = src[2 * pair, low:low + 4, :]
            out[19 + pair, 4:8] = src[2 * pair + 1, low:low + 4, :]
        out[27] = reg[0].astype(F32)
        out[28] = msk[0].astype(F32)


def segments(block):
    found = []
    for row in range(WR):
        start = (WC * (row - RING)) % LANES
        begin, end = max(start, 128 * block), min(start + WC, 128 * block + 128)
        if begin < end:
            found.append((begin - 128 * block, row))
    return sorted(found)


def residual_kernel(it, zlo, zhi, lo, hi, src, reg, msk, chunks, nu, resid, field, rows):
    group = lax.axis_index("gz")
    mid = slice(8, 8 + YC)
    field[0, mid] = zlo[0]
    field[1:17, mid] = it[...]
    field[17:19, mid] = zhi[...]
    field[:, 0:8] = lo[0:19]
    field[:, 8 + YC:] = hi[0:19]
    region = jnp.concatenate([lo[27], reg[0].astype(F32), hi[27]], axis=0)
    fixed = jnp.concatenate([lo[28], msk[0].astype(F32), hi[28]], axis=0)
    lane = lane_iota((FR, 128))
    first, last = lane == 0, lane == 127
    iron, copper, held = region == 2.0, region == 1.0, fixed == 1.0

    def nu_plane(p, total):
        u = field[p]
        dz = field[p + 1] - u
        dy = roll(u, -1, 0) - u
        dx = jnp.where(last, 0.0, roll(u, -1, 1)) - u
        bsq = dz * dz + dy * dy + dx * dx
        bsq = bsq * bsq
        outside = ((p == 0) & (group == 0)) | ((p == 17) & (group == GZ - 1))
        value = jnp.where(iron, 0.05 + bsq / (bsq + 9.0), 1.0)
        value = jnp.where(outside, 1.0, value)
        nu[p] = value
        inner = (p > 0) & (p < 17)
        return total + jnp.where(inner, value, 0.0)

    total = lax.fori_loop(0, 18, nu_plane, jnp.zeros((FR, 128), F32))

    def resid_plane(z, carry):
        u, n = field[z + 1], nu[z + 1]
        uz, nz = field[z + 2], nu[z + 2]
        ub, nb = field[z], nu[z]
        flow = 0.5 * (n + nz) * (u - uz) + 0.5 * (n + nb) * (u - ub)
        fy = 0.5 * (n + roll(n, -1, 0)) * (u - roll(u, -1, 0))
        flow = flow + (fy - roll(fy, 1, 0))
        nx = jnp.where(last, 1.0, roll(n, -1, 1))
        ux = jnp.where(last, 0.0, roll(u, -1, 1))
        fx = 0.5 * (n + nx) * (u - ux)
        flow = flow + (fx - jnp.where(first, -0.5 * (n + 1.0) * u, roll(fx, 1, 1)))
        half = 4 * lax.rem(z, 2)
        before = lo[19 + lax.div(z, 2), pl.ds(half, 4), :]
        after = hi[19 + lax.div(z, 2), pl.ds(half, 4), :]
        drive = jnp.concatenate([before, before, src[z], after, after], axis=0)
        value = -jnp.where(held, u, flow - jnp.where(copper, drive, 0.0))
        rows[pl.ds(pl.multiple_of(z * FR, FR), FR), :] = value
        resid[z] = value[mid]
        return carry

    lax.fori_loop(0, ZC, resid_plane, 0)
    faces = 2.0 * total + 0.5 * (
        roll(total, -1, 0) + roll(total, 1, 0)
        + jnp.where(last, float(ZC), roll(total, -1, 1))
        + jnp.where(first, float(ZC), roll(total, 1, 1))
    )
    rows[16 * FR:17 * FR, :] = total
    rows[17 * FR:18 * FR, :] = faces
    rows[18 * FR:24 * FR, :] = jnp.zeros((6 * FR, 128), F32)

    lane = lane_iota((8, 128))
    for yp in range(YP):
        for tile in range(3):
            turned = []
            for row in range(WR):
                at = ROW0[yp] + row + 4
                line = rows[pl.ds(8 * tile * FR + at, 8, stride=FR), :]
                turned.append(roll(line, WC * (row - RING) + RING, 1))
            for block in range(4):
                parts = segments(block)
                for xp in range(XP):
                    place = (lane - 16 * xp) & 127
                    value = turned[parts[0][1]]
                    for begin, row in parts[1:]:
                        value = jnp.where(place >= begin, turned[row], value)
                    value = roll(value, -16 * xp, 1)
                    if tile < 2:
                        at = 16 * block + 8 * tile
                        chunks[yp * XP + xp, at:at + 8, :] = value
                    else:
                        at = 64 + 2 * block
                        chunks[yp * XP + xp, at:at + 2, :] = value[0:2]


def product(high, low, right_high, right_low):
    dot = functools.partial(jnp.dot, preferred_element_type=F32)
    return dot(high, right_high) + (dot(high, right_low) + dot(low, right_high))


def modes_kernel(got, high, low, lam, out, lines, smooth_high, smooth_low, back):
    group, column = lax.axis_index("gz"), lax.axis_index("gy")
    yp, xp = lax.div(group, XP), lax.rem(group, XP)
    s_high, s_low = high[...], low[...]
    for block in range(4):
        value = got[:, 16 * block:16 * block + 16, :].reshape(NZ, 128)
        v_high = value.astype(BF16)
        v_low = (value - v_high.astype(F32)).astype(BF16)
        lines[:, 128 * block:128 * block + 128] = product(s_high, s_low, v_high, v_low)

    sums = jnp.sum(got[:, 64:72, :], axis=0) * (1.0 / NZ)
    mean = jnp.concatenate([sums[2 * b:2 * b + 1] for b in range(4)], axis=1)
    faces = jnp.concatenate([sums[2 * b + 1:2 * b + 2] for b in range(4)], axis=1)
    spot = (lane_iota((1, LANES)) + RING * WC) & (LANES - 1)
    row = (spot * 2979) >> 16
    col = spot - row * WC
    ypos = column * YC + 16 * yp + jnp.where(yp > 0, 1, 0) + row - 4
    xpos = 16 * xp - RING + col
    inside = (row < WR) & (xpos >= 0) & (xpos < NX) & (ypos >= 0) & (ypos < NY)
    right = 0.5 * (mean + roll(mean, -1, 1))
    left = roll(right, 1, 1)
    above = 0.5 * (mean + roll(mean, -WC, 1))
    below = roll(above, WC, 1)

    def smooth(step, carry):
        at = pl.ds(pl.multiple_of(step * 32, 32), 32)
        vhat = lines[at, :]
        lam_rows = lam[at, :]
        lam_rows = jnp.concatenate([lam_rows] * 4, axis=1)
        factor = jnp.where(inside, 0.6 / (faces + lam_rows * mean), 0.0)
        w = factor * vhat
        for _ in range(3):
            near = (
                above * roll(w, -WC, 1) + below * roll(w, WC, 1)
                + right * roll(w, -1, 1) + left * roll(w, 1, 1)
            )
            w = 0.4 * w + factor * (vhat + near)
        w = w[:, :384]
        w_high = w.astype(BF16)
        smooth_high[at, :] = w_high
        smooth_low[at, :] = (w - w_high.astype(F32)).astype(BF16)
        return carry

    lax.fori_loop(0, NZ // 32, smooth, 0)

    spot = lane_iota((384, 384))
    own = jnp.where(yp == 0, 1, 0)
    halo = jnp.where(yp == 0, 0, 16)
    pick = jnp.where(spot < 256, own + (spot >> 4), halo) * WC + RING + (spot & 15)
    choose = jnp.where(lax.broadcasted_iota(jnp.int32, (384, 384), 0) == pick, 1.0, 0.0)
    choose = choose.astype(BF16)
    w_high = jnp.dot(smooth_high[...], choose, preferred_element_type=F32).astype(BF16)
    w_low = jnp.dot(smooth_low[...], choose, preferred_element_type=F32).astype(BF16)
    back[8:8 + NZ, :] = product(s_high, s_low, w_high, w_low)
    back[0:8, :] = jnp.zeros((8, 384), F32)
    back[8 + NZ:, :] = jnp.zeros((8, 384), F32)

    sub = lax.broadcasted_iota(jnp.int32, (8, 128), 0)
    pattern = (((lane_iota((8, 128)) >> 4) + sub) & 7) == 0
    for peer in range(GZ):
        at = 8 + ZC * peer
        for block in range(2):
            lanes = slice(128 * block, 128 * block + 128)
            out[peer, 16 * block:16 * block + 16, :] = back[at:at + ZC, lanes]
            out[peer, 32 + block:33 + block, :] = back[at - 1:at, lanes]
            out[peer, 34 + block:35 + block, :] = back[at + ZC:at + ZC + 1, lanes]
            piece = back[at + 8 * block:at + 8 * block + 8, 256:384]
            piece = jnp.sum(jnp.where(pattern, piece, 0.0), axis=0, keepdims=True)
            out[peer, 36 + block:37 + block, :] = piece
        out[peer, 38:40, :] = jnp.zeros((2, 128), F32)


def image_kernel(got, nu, resid, msk, zdir, image, sums, frame):
    lane = lane_iota((8, 128))
    places = [(lane >> 4) == k for k in range(8)]

    def spread(tiles, jj):
        value = tiles[0]
        for xp in range(1, XP):
            value = jnp.where(places[(jj + xp) % 8], tiles[xp], value)
        return roll(value, -16 * jj, 1)

    for yp in range(YP):
        for block in range(2):
            for tile in range(2):
                at = 16 * block + 8 * tile
                tiles = [
                    roll(got[yp * XP + xp, at:at + 8, :], 16 * xp, 1) for xp in range(XP)
                ]
                for jj in range(8):
                    y = 8 + 16 * yp + 8 * block + jj
                    frame[pl.ds((1 + 8 * tile) * FR + y, 8, stride=FR), :] = spread(tiles, jj)
        tiles = [roll(got[yp * XP + xp, 32:40, :], 16 * xp, 1) for xp in range(XP)]
        for jj in range(8):
            value = spread(tiles, jj)
            y = 8 + 16 * yp + jj
            for k in range(2):
                frame[y + 8 * k:y + 8 * k + 1, :] = value[k:k + 1]
                at = 17 * FR + y + 8 * k
                frame[at:at + 1, :] = value[2 + k:3 + k]

    sub = lax.broadcasted_iota(jnp.int32, (8, 128), 0)
    turn = ((lane >> 4) + sub) & 7
    for yp, y in ((0, 7), (YP - 1, 8 + YC)):
        for tile in range(2):
            value = jnp.zeros((8, 128), F32)
            for xp in range(XP):
                line = got[yp * XP + xp, 36 + tile:37 + tile, :]
                line = roll(jnp.broadcast_to(line, (8, 128)), 16 * xp, 1)
                value = jnp.where(turn == xp, line, value)
            value = pltpu.roll(value, 0, 1, stride=16, stride_axis=0)
            frame[pl.ds((1 + 8 * tile) * FR + y, 8, stride=FR), :] = value

    lane = lane_iota((YC, 128))
    first, last = lane == 0, lane == 127
    held = msk[0] == 1

    def plane(z, carry):
        at = (z + 1) * FR + 8
        d, n = frame[pl.ds(at, YC), :], nu[z + 1, 8:8 + YC]

        def flux(shift, other):
            return 0.5 * (n + other) * (d - frame[pl.ds(at + shift, YC), :])

        flow = flux(FR, nu[z + 2, 8:8 + YC]) + flux(-FR, nu[z, 8:8 + YC])
        flow = flow + flux(1, nu[z + 1, 9:9 + YC]) + flux(-1, nu[z + 1, 7:7 + YC])
        nx = jnp.where(last, 1.0, roll(n, -1, 1))
        dx = jnp.where(last, 0.0, roll(d, -1, 1))
        fx = 0.5 * (n + nx) * (d - dx)
        flow = flow + (fx - jnp.where(first, -0.5 * (n + 1.0) * d, roll(fx, 1, 1)))
        value = jnp.where(held, d, flow)
        zdir[z] = d
        image[z] = value
        r = resid[z]
        rr, ri, ii = carry
        return rr + r * r, ri + r * value, ii + value * value

    zero = jnp.zeros((YC, 128), F32)
    parts = lax.fori_loop(0, ZC, plane, (zero, zero, zero))
    line = lane_iota((1, 128))
    packed = jnp.zeros((1, 128), F32)
    for k, part in enumerate(parts):
        packed = jnp.where(line == k, jnp.sum(part), packed)
    sums[...] = jnp.broadcast_to(packed[None], sums.shape)


def output_kernel(sums, zdir, image, resid, correction, lin_residual, rms):
    total = jnp.sum(sums[...], axis=0)
    beta_sq = total[0:1, 0:1] + 1e-06
    beta = jnp.sqrt(beta_sq)
    h_one = total[0:1, 1:2] / beta_sq
    denom = total[0:1, 2:3] / beta_sq - h_one * h_one * (1e-06 / beta_sq) + 1e-06
    gamma = h_one / denom
    correction[...] = zdir[...] * gamma[None]
    lin_residual[...] = resid[...] - gamma[None] * image[...]
    rms[...] = jnp.broadcast_to(beta * (1.0 / np.sqrt(float(NZ * NY * NX))), rms.shape)


def call(kernel, out_shape, scratch=(), in_specs=None):
    extra = {} if in_specs is None else {"in_specs": in_specs, "grid": (1,)}
    return pl.pallas_call(
        kernel,
        out_shape=out_shape,
        scratch_shapes=scratch,
        compiler_params=pltpu.CompilerParams(vmem_limit_bytes=VMEM_LIMIT),
        **extra,
    )


def struct(*shape):
    return jax.ShapeDtypeStruct(shape, F32)


def whole(*shape):
    return pl.BlockSpec(shape, lambda i: (0,) * len(shape))


def shards(iterate, source, region, fixed_mask):
    up_z = [(i, i + 1) for i in range(GZ - 1)]
    down_z = [(i + 1, i) for i in range(GZ - 1)]
    up_y = [(i, i + 1) for i in range(GY - 1)]
    down_y = [(i + 1, i) for i in range(GY - 1)]
    zlo = lax.ppermute(iterate[ZC - 1:ZC], "gz", up_z)
    zhi = lax.ppermute(iterate[0:2], "gz", down_z)

    def edge(planes, place):
        return pl.BlockSpec((planes, 8, 128), lambda i: (0, place, 0))

    both = [edge(ZC, 0), edge(ZC, YC // 8 - 1)]
    flat = [edge(1, 0), edge(1, YC // 8 - 1)]
    down, up = call(
        halo_pack,
        (struct(29, 8, 128), struct(29, 8, 128)),
        in_specs=both + [whole(1, YC, 128), whole(2, YC, 128)] + both + flat + flat,
    )(iterate, iterate, zlo, zhi, source, source, region, region, fixed_mask, fixed_mask)
    lo = lax.ppermute(up, "gy", up_y)
    hi = lax.ppermute(down, "gy", down_y)

    cells = (ZC, YC, 128)
    chunks, nu, resid = call(
        residual_kernel,
        (struct(GZ, 72, 128), struct(18, FR, 128), struct(*cells)),
        scratch=[pltpu.VMEM((19, FR, 128), F32), pltpu.VMEM((24 * FR, 128), F32)],
        in_specs=[
            whole(*cells), whole(1, YC, 128), whole(2, YC, 128), whole(29, 8, 128),
            whole(29, 8, 128), whole(*cells), whole(1, YC, 128), whole(1, YC, 128),
        ],
    )(iterate, zlo, zhi, lo, hi, source, region, fixed_mask)
    windows = lax.all_to_all(chunks, "gz", 0, 0, tiled=True)
    high, low, lam = tables()
    sent = call(
        modes_kernel,
        struct(GZ, 40, 128),
        scratch=[
            pltpu.VMEM((NZ, LANES), F32), pltpu.VMEM((NZ, 384), BF16),
            pltpu.VMEM((NZ, 384), BF16), pltpu.VMEM((NZ + 16, 384), F32),
        ],
    )(windows, jnp.asarray(high), jnp.asarray(low), jnp.asarray(lam))
    returned = lax.all_to_all(sent, "gz", 0, 0, tiled=True)
    zdir, image, sums = call(
        image_kernel,
        (struct(*cells), struct(*cells), struct(GZ * GY, 1, 128)),
        scratch=[pltpu.VMEM((18 * FR, 128), F32)],
        in_specs=[
            whole(GZ, 40, 128), whole(18, FR, 128), whole(*cells), whole(1, YC, 128),
        ],
    )(returned, nu, resid, fixed_mask)
    sums = lax.all_to_all(sums, ("gz", "gy"), 0, 0, tiled=True)
    correction, lin_residual, rms = call(
        output_kernel, (struct(*cells), struct(*cells), struct(1, 128))
    )(sums, zdir, image, resid)
    return correction, lin_residual, rms[0, 0]


def solution(mesh):
    placed = (P("gz", "gy", None),) * 4
    return jax.shard_map(
        shards,
        mesh=mesh,
        in_specs=placed,
        out_specs=(P("gz", "gy", None), P("gz", "gy", None), P()),
        check_vma=False,
    )
```

```python
import functools

import jax
import jax.numpy as jnp
import ml_dtypes
import numpy as np
from jax import lax
from jax.experimental import pallas as pl
from jax.experimental.pallas import tpu as pltpu
from jax.sharding import PartitionSpec as P

F32 = jnp.float32
BF16 = jnp.bfloat16
NZ, NY, NX = 512, 256, 128
GZ, GY = 32, 4
ZC, YC = NZ // GZ, NY // GY
FR = YC + 16
WR, WC, RING = 23, 22, 3
LANES = 512
YP, XP = 4, 8
ROW0 = (0, 17, 33, 49)
VMEM_LIMIT = 40 * 1024 * 1024


def tables():
    index = np.arange(NZ, dtype=np.int64)
    phase = (index[:, None] + 1) * (index[None, :] + 1) % (2 * (NZ + 1))
    table = np.sqrt(2.0 / (NZ + 1)) * np.sin(np.pi * phase / (NZ + 1))
    table = table.astype(np.float32)
    high = table.astype(ml_dtypes.bfloat16)
    low = (table - high.astype(np.float32)).astype(ml_dtypes.bfloat16)
    lam = 2.0 - 2.0 * np.cos(np.pi * (index + 1.0) / (NZ + 1))
    lam = np.broadcast_to(lam.astype(np.float32)[:, None], (NZ, 128))
    return np.roll(high, 2, 1), np.roll(low, 2, 1), high, low, np.ascontiguousarray(lam)


def lane_iota(shape):
    return lax.broadcasted_iota(jnp.int32, shape, len(shape) - 1)


def roll(value, shift, axis):
    return pltpu.roll(value, shift % value.shape[axis], axis)


def edge_kernel(it, src, reg, msk, zmsg, up, down, it_out, src_out, reg_out, msk_out,
                e_it, e_src, e_reg, e_msk, sems):
    copies = [(it.at[ZC - 3:ZC], zmsg.at[0:3]), (src.at[ZC - 2:ZC], zmsg.at[3:5])]
    for side, row in enumerate((0, YC - 8)):
        rows = pl.ds(row, 8)
        copies += [
            (it.at[:, rows], e_it.at[side]),
            (src.at[:, rows], e_src.at[side]),
            (reg.at[0:1, rows], e_reg.at[side]),
            (msk.at[0:1, rows], e_msk.at[side]),
        ]
    copies += [
        (it, it_out), (src.at[0:ZC - 2], src_out), (reg.at[0:1], reg_out), (msk.at[0:1], msk_out),
    ]
    copies = [pltpu.make_async_copy(x, y, sems.at[k]) for k, (x, y) in enumerate(copies)]
    for copy in copies:
        copy.start()
    for copy in copies[:-4]:
        copy.wait()
    for z in range(ZC):
        up[5 * z:5 * z + 5] = e_it[1, z, 3:8]
        down[6 * z:6 * z + 6] = e_it[0, z, 0:6]
    for z in range(ZC - 2):
        up[80 + 4 * z:84 + 4 * z] = e_src[1, z, 4:8]
        down[96 + 4 * z:100 + 4 * z] = e_src[0, z, 0:4]
    up[136:141] = e_reg[1, 0, 3:8].astype(F32)
    up[141:145] = e_msk[1, 0, 4:8].astype(F32)
    up[145:152] = jnp.zeros((7, 128), F32)
    down[152:157] = e_reg[0, 0, 0:5].astype(F32)
    down[157:161] = e_msk[0, 0, 0:4].astype(F32)
    down[161:168] = jnp.zeros((7, 128), F32)
    for copy in copies[-4:]:
        copy.wait()


def corner_kernel(zgot, up, down):
    for p in range(3):
        up[5 * p:5 * p + 5] = zgot[p, YC - 5:YC]
        down[6 * p:6 * p + 6] = zgot[p, 0:6]
    for q in range(2):
        up[15 + 4 * q:19 + 4 * q] = zgot[3 + q, YC - 4:YC]
        down[18 + 4 * q:22 + 4 * q] = zgot[3 + q, 0:4]
    up[23:24] = jnp.zeros((1, 128), F32)
    down[26:32] = jnp.zeros((6, 128), F32)


def segments(block):
    found = []
    for row in range(WR):
        start = (WC * (row - RING)) % LANES
        begin, end = max(start, 128 * block), min(start + WC, 128 * block + 128)
        if begin < end:
            found.append((begin - 128 * block, row))
    return sorted(found)


def residual_kernel(it, src, reg, msk, zgot, lo, hi, corner_lo, corner_hi,
                    chunks, nu, resid, message, field, drive, flat, rows):
    group, column = lax.axis_index("gz"), lax.axis_index("gy")
    low_end, high_end = column == 0, column == GY - 1
    start = group == 0
    mid = slice(8, 8 + YC)

    def below(value):
        return jnp.where(low_end, 0.0, value)

    def above(value):
        return jnp.where(high_end, 0.0, value)

    for p in range(19):
        z = p - 3
        field[p, mid] = zgot[p] if p < 3 else it[z]
        field[p, 3:8] = below(
            corner_lo[5 * p:5 * p + 5] if p < 3 else lo[5 * z:5 * z + 5]
        )
        field[p, 72:78] = above(
            corner_hi[6 * p:6 * p + 6] if p < 3 else hi[6 * z:6 * z + 6]
        )
    for t in range(ZC):
        z = t - 2
        drive[t, mid] = zgot[3 + t] if t < 2 else src[z]
        drive[t, 4:8] = (
            corner_lo[15 + 4 * t:19 + 4 * t] if t < 2 else lo[80 + 4 * z:84 + 4 * z]
        )
        drive[t, 72:76] = (
            corner_hi[18 + 4 * t:22 + 4 * t] if t < 2 else hi[96 + 4 * z:100 + 4 * z]
        )
    flat[0, mid] = reg[0].astype(F32)
    flat[0, 3:8] = below(lo[136:141])
    flat[0, 72:77] = above(hi[152:157])
    flat[1, mid] = msk[0].astype(F32)
    flat[1, 4:8] = lo[141:145]
    flat[1, 72:76] = hi[157:161]
    region, fixed = flat[0], flat[1]
    lane = lane_iota((FR, 128))
    first, last = lane == 0, lane == 127
    iron, copper, held = region == 2.0, region == 1.0, fixed == 1.0

    for p in range(18):
        u = field[p]
        uz = field[p + 1]
        if p == 2:
            uz = jnp.where(start, 0.0, uz)
        dz = uz - u
        dy = roll(u, -1, 0) - u
        dx = jnp.where(last, 0.0, roll(u, -1, 1)) - u
        bsq = dz * dz + dy * dy + dx * dx
        bsq = bsq * bsq
        nu[p] = jnp.where(iron, 0.05 + bsq / (bsq + 9.0), 1.0)

    total = nu[1]
    for p in range(2, 17):
        total = total + nu[p]
    flux = 0.5 * (nu[0] + nu[1]) * (field[0] - field[1])
    for t in range(ZC):
        p = t + 1
        u, n = field[p], nu[p]
        uz, nz = field[p + 1], nu[p + 1]
        if p == 2:
            uz, nz = jnp.where(start, 0.0, uz), jnp.where(start, 1.0, nz)
        if p == 3:
            flux = jnp.where(start, -0.5 * (1.0 + n) * u, flux)
        ahead = 0.5 * (n + nz) * (u - uz)
        flow = ahead - flux
        flux = ahead
        fy = 0.5 * (n + roll(n, -1, 0)) * (u - roll(u, -1, 0))
        flow = flow + (fy - roll(fy, 1, 0))
        nx = jnp.where(last, 1.0, roll(n, -1, 1))
        ux = jnp.where(last, 0.0, roll(u, -1, 1))
        fx = 0.5 * (n + nx) * (u - ux)
        flow = flow + (fx - jnp.where(first, -0.5 * (n + 1.0) * u, roll(fx, 1, 1)))
        value = -jnp.where(held, u, flow - jnp.where(copper, drive[t], 0.0))
        rows[t * FR:t * FR + FR, :] = value
        if t < 2:
            message[3 * FR + YC * t:3 * FR + YC * t + YC, :] = value[mid]
        else:
            resid[t - 2] = value[mid]
    for k in range(3):
        message[FR * k:FR * k + FR, :] = nu[1 + k]

    faces = 2.0 * total + 0.5 * (
        roll(total, -1, 0) + roll(total, 1, 0)
        + jnp.where(last, float(ZC), roll(total, -1, 1))
        + jnp.where(first, float(ZC), roll(total, 1, 1))
    )
    rows[16 * FR:17 * FR, :] = total
    rows[17 * FR:18 * FR, :] = faces
    rows[18 * FR:24 * FR, :] = jnp.zeros((6 * FR, 128), F32)

    lane = lane_iota((8, 128))
    places = [(lane - 16 * xp) & 127 for xp in range(XP)]
    for yp in range(YP):
        for block in range(4):
            parts = segments(block)
            lines = []
            for begin, row in parts:
                at = ROW0[yp] + row + 4
                lines.append([
                    roll(
                        rows[pl.ds(8 * tile * FR + at, 8, stride=FR), :],
                        WC * (row - RING) + RING, 1,
                    )
                    for tile in range(3)
                ])
            for xp in range(XP):
                values = lines[0]
                for (begin, row), line in zip(parts[1:], lines[1:]):
                    later = places[xp] >= begin
                    values = [jnp.where(later, x, y) for x, y in zip(line, values)]
                values = [roll(value, -16 * xp, 1) for value in values]
                peer, at = yp * XP + xp, 16 * block
                chunks[peer, at:at + 8, :] = values[0]
                chunks[peer, at + 8:at + 16, :] = values[1]
                chunks[peer, 64 + 2 * block:66 + 2 * block, :] = values[2][0:2]


def product(high, low, right_high, right_low):
    left = jnp.concatenate([high, low, high], axis=1)
    right = jnp.concatenate([right_high, right_high, right_low], axis=0)
    return jnp.dot(left, right, preferred_element_type=F32)


def modes_kernel(got, ahead_high, ahead_low, high, low, lam, out, lines, back):
    group, column = lax.axis_index("gz"), lax.axis_index("gy")
    yp, xp = lax.div(group, XP), lax.rem(group, XP)
    s_high, s_low = ahead_high[...], ahead_low[...]
    for half in range(2):
        value = jnp.concatenate(
            [
                got[:, 16 * block:16 * block + 16, :].reshape(NZ, 128)
                for block in (2 * half, 2 * half + 1)
            ],
            axis=1,
        )
        v_high = value.astype(BF16)
        v_low = (value - v_high.astype(F32)).astype(BF16)
        lines[:, 256 * half:256 * half + 256] = product(s_high, s_low, v_high, v_low)

    sums = jnp.sum(got[:, 64:72, :], axis=0) * (1.0 / NZ)
    mean = jnp.concatenate([sums[2 * b:2 * b + 1] for b in range(4)], axis=1)
    faces = jnp.concatenate([sums[2 * b + 1:2 * b + 2] for b in range(4)], axis=1)
    spot = (lane_iota((1, LANES)) + RING * WC) & (LANES - 1)
    row = (spot * 2979) >> 16
    col = spot - row * WC
    ypos = column * YC + 16 * yp + jnp.where(yp > 0, 1, 0) + row - 4
    xpos = 16 * xp - RING + col
    inside = (row < WR) & (xpos >= 0) & (xpos < NX) & (ypos >= 0) & (ypos < NY)
    right = 0.5 * (mean + roll(mean, -1, 1))
    left = roll(right, 1, 1)
    above = 0.5 * (mean + roll(mean, -WC, 1))
    below = roll(above, WC, 1)

    vhat = lines[...]
    lam_rows = jnp.concatenate([lam[...]] * 4, axis=1)
    factor = jnp.where(inside, 0.6 / (faces + lam_rows * mean), 0.0)
    w = factor * vhat
    for _ in range(3):
        near = (
            above * roll(w, -WC, 1) + below * roll(w, WC, 1)
            + right * roll(w, -1, 1) + left * roll(w, 1, 1)
        )
        w = 0.4 * w + factor * (vhat + near)
    w = w[:, :384]
    w_high = w.astype(BF16)
    w_low = (w - w_high.astype(F32)).astype(BF16)

    spot = lane_iota((384, 384))
    own = jnp.where(yp == 0, 1, 0)
    halo = jnp.where(yp == 0, 0, 16)
    pick = jnp.where(spot < 256, own + (spot >> 4), halo) * WC + RING + (spot & 15)
    choose = jnp.where(lax.broadcasted_iota(jnp.int32, (384, 384), 0) == pick, 1.0, 0.0)
    choose = choose.astype(BF16)
    s_high, s_low = high[...], low[...]
    w_high = jnp.dot(w_high, choose, preferred_element_type=F32).astype(BF16)
    w_low = jnp.dot(w_low, choose, preferred_element_type=F32).astype(BF16)
    back[8:8 + NZ, :] = product(s_high, s_low, w_high, w_low)
    back[0:8, :] = jnp.zeros((8, 384), F32)
    back[8 + NZ:, :] = jnp.zeros((8, 384), F32)

    sub = lax.broadcasted_iota(jnp.int32, (8, 128), 0)
    pattern = (((lane_iota((8, 128)) >> 4) + sub) & 7) == 0
    for peer in range(GZ):
        at = 8 + ZC * peer
        for block in range(2):
            lanes = slice(128 * block, 128 * block + 128)
            out[peer, 16 * block:16 * block + 16, :] = back[at:at + ZC, lanes]
            out[peer, 32 + block:33 + block, :] = back[at - 1:at, lanes]
            out[peer, 34 + block:35 + block, :] = back[at + ZC:at + ZC + 1, lanes]
            piece = back[at + 8 * block:at + 8 * block + 8, 256:384]
            piece = jnp.sum(jnp.where(pattern, piece, 0.0), axis=0, keepdims=True)
            out[peer, 36 + block:37 + block, :] = piece
        out[peer, 38:40, :] = jnp.zeros((2, 128), F32)


def resid_plane(resid, message, z):
    if z < ZC - 2:
        return resid[z]
    at = 3 * FR + YC * (z - ZC + 2)
    return message[at:at + YC, :]


def image_kernel(got, nu, resid, message, msk, zdir, image, sums, frame):
    lane = lane_iota((8, 128))
    places = [(lane >> 4) == k for k in range(8)]

    def spread(tiles, jj):
        value = tiles[0]
        for xp in range(1, XP):
            value = jnp.where(places[(jj + xp) % 8], tiles[xp], value)
        return roll(value, -16 * jj, 1)

    for yp in range(YP):
        for block in range(2):
            for tile in range(2):
                at = 16 * block + 8 * tile
                tiles = [
                    roll(got[yp * XP + xp, at:at + 8, :], 16 * xp, 1) for xp in range(XP)
                ]
                for jj in range(8):
                    y = 8 + 16 * yp + 8 * block + jj
                    frame[pl.ds((1 + 8 * tile) * FR + y, 8, stride=FR), :] = spread(tiles, jj)
        tiles = [roll(got[yp * XP + xp, 32:40, :], 16 * xp, 1) for xp in range(XP)]
        for jj in range(8):
            value = spread(tiles, jj)
            y = 8 + 16 * yp + jj
            for k in range(2):
                frame[y + 8 * k:y + 8 * k + 1, :] = value[k:k + 1]
                at = 17 * FR + y + 8 * k
                frame[at:at + 1, :] = value[2 + k:3 + k]

    sub = lax.broadcasted_iota(jnp.int32, (8, 128), 0)
    turn = ((lane >> 4) + sub) & 7
    for yp, y in ((0, 7), (YP - 1, 8 + YC)):
        for tile in range(2):
            value = jnp.zeros((8, 128), F32)
            for xp in range(XP):
                line = got[yp * XP + xp, 36 + tile:37 + tile, :]
                line = roll(jnp.broadcast_to(line, (8, 128)), 16 * xp, 1)
                value = jnp.where(turn == xp, line, value)
            value = pltpu.roll(value, 0, 1, stride=16, stride_axis=0)
            frame[pl.ds((1 + 8 * tile) * FR + y, 8, stride=FR), :] = value

    lane = lane_iota((YC, 128))
    first, last = lane == 0, lane == 127
    held = msk[0] == 1

    group = lax.axis_index("gz")

    def nu_rows(z, shift):
        at = 8 + shift
        if z >= ZC - 2:
            value = message[FR * (z - ZC + 2) + at:FR * (z - ZC + 2) + at + YC, :]
        else:
            value = nu[z + 3, at:at + YC]
        if z == -1:
            value = jnp.where(group == 0, 1.0, value)
        if z == ZC:
            value = jnp.where(group == GZ - 1, 1.0, value)
        return value

    def dir_rows(z, shift):
        at = (z + 1) * FR + 8 + shift
        return frame[at:at + YC, :]

    d, n = dir_rows(0, 0), nu_rows(0, 0)
    flux = 0.5 * (nu_rows(-1, 0) + n) * (dir_rows(-1, 0) - d)
    rr = ri = ii = jnp.zeros((8, 128), F32)

    def fold(value):
        return jnp.sum(value.reshape(YC // 8, 8, 128), axis=0)

    for z in range(ZC):
        dz, nz = dir_rows(z + 1, 0), nu_rows(z + 1, 0)
        ahead = 0.5 * (n + nz) * (d - dz)
        flow = ahead - flux
        flow = flow + 0.5 * (n + nu_rows(z, 1)) * (d - dir_rows(z, 1))
        flow = flow + 0.5 * (n + nu_rows(z, -1)) * (d - dir_rows(z, -1))
        nx = jnp.where(last, 1.0, roll(n, -1, 1))
        dx = jnp.where(last, 0.0, roll(d, -1, 1))
        fx = 0.5 * (n + nx) * (d - dx)
        flow = flow + (fx - jnp.where(first, -0.5 * (n + 1.0) * d, roll(fx, 1, 1)))
        value = jnp.where(held, d, flow)
        zdir[z] = d
        image[z] = value
        r = resid_plane(resid, message, z)
        rr, ri, ii = rr + fold(r * r), ri + fold(r * value), ii + fold(value * value)
        d, n, flux = dz, nz, ahead

    parts = (rr, ri, ii)
    line = lane_iota((1, 128))
    packed = jnp.zeros((1, 128), F32)
    for k, part in enumerate(parts):
        packed = jnp.where(line == k, jnp.sum(part), packed)
    sums[...] = jnp.broadcast_to(packed[None], sums.shape)


def output_kernel(sums, zdir, image, resid, message, correction, lin_residual, rms):
    total = jnp.sum(sums[...], axis=0)
    beta_sq = total[0:1, 0:1] + 1e-06
    beta = jnp.sqrt(beta_sq)
    h_one = total[0:1, 1:2] / beta_sq
    denom = total[0:1, 2:3] / beta_sq - h_one * h_one * (1e-06 / beta_sq) + 1e-06
    gamma = h_one / denom
    correction[...] = zdir[...] * gamma[None]
    for z in range(ZC):
        lin_residual[z] = resid_plane(resid, message, z) - gamma * image[z]
    rms[...] = jnp.broadcast_to(beta * (1.0 / np.sqrt(float(NZ * NY * NX))), rms.shape)


def call(kernel, out_shape, scratch=(), in_specs=None):
    extra = {} if in_specs is None else {"in_specs": in_specs}
    return pl.pallas_call(
        kernel,
        out_shape=out_shape,
        scratch_shapes=scratch,
        compiler_params=pltpu.CompilerParams(vmem_limit_bytes=VMEM_LIMIT),
        **extra,
    )


def struct(*shape):
    return jax.ShapeDtypeStruct(shape, F32)


def cyclic(count, step):
    return [(i, (i + step) % count) for i in range(count)]


def shards(iterate, source, region, fixed_mask):
    far = [pl.BlockSpec(memory_space=pltpu.HBM)] * 4
    arguments = [
        pltpu.with_memory_space_constraint(argument, pltpu.HBM)
        for argument in (iterate, source, region, fixed_mask)
    ]
    edge = (2, ZC, 8, 128)
    flat = jax.ShapeDtypeStruct((1, YC, 128), jnp.int32)
    zmsg, up, down, it, src, reg, msk = call(
        edge_kernel,
        (
            struct(5, YC, 128), struct(152, 128), struct(168, 128),
            struct(ZC, YC, 128), struct(ZC - 2, YC, 128), flat, flat,
        ),
        scratch=[
            pltpu.VMEM(edge, F32), pltpu.VMEM(edge, F32),
            pltpu.VMEM((2, 1, 8, 128), jnp.int32), pltpu.VMEM((2, 1, 8, 128), jnp.int32),
            pltpu.SemaphoreType.DMA((14,)),
        ],
        in_specs=far,
    )(*arguments)
    zgot = lax.ppermute(zmsg, "gz", cyclic(GZ, 1))
    lo = lax.ppermute(up, "gy", cyclic(GY, 1))
    hi = lax.ppermute(down, "gy", cyclic(GY, -1))
    corner_up, corner_down = call(corner_kernel, (struct(24, 128), struct(32, 128)))(zgot)
    corner_lo = lax.ppermute(corner_up, "gy", cyclic(GY, 1))
    corner_hi = lax.ppermute(corner_down, "gy", cyclic(GY, -1))

    cells = (ZC, YC, 128)
    chunks, nu, resid, message = call(
        residual_kernel,
        (
            struct(GZ, 72, 128), struct(18, FR, 128), struct(ZC - 2, YC, 128),
            struct(3 * FR + 2 * YC, 128),
        ),
        scratch=[
            pltpu.VMEM((19, FR, 128), F32), pltpu.VMEM((ZC, FR, 128), F32),
            pltpu.VMEM((2, FR, 128), F32), pltpu.VMEM((24 * FR, 128), F32),
        ],
    )(it, src, reg, msk, zgot, lo, hi, corner_lo, corner_hi)
    message = lax.ppermute(message, "gz", cyclic(GZ, -1))
    windows = lax.all_to_all(chunks, "gz", 0, 0, tiled=True)
    sent = call(
        modes_kernel,
        struct(GZ, 40, 128),
        scratch=[
            pltpu.VMEM((NZ, LANES), F32), pltpu.VMEM((NZ + 16, 384), F32),
        ],
    )(windows, *[jnp.asarray(table) for table in tables()])
    returned = lax.all_to_all(sent, "gz", 0, 0, tiled=True)
    zdir, image, sums = call(
        image_kernel,
        (struct(*cells), struct(*cells), struct(GZ * GY, 1, 128)),
        scratch=[pltpu.VMEM((18 * FR, 128), F32)],
    )(returned, nu, resid, message, msk)
    sums = lax.all_to_all(sums, ("gz", "gy"), 0, 0, tiled=True)
    correction, lin_residual, rms = call(
        output_kernel, (struct(*cells), struct(*cells), struct(1, 128))
    )(sums, zdir, image, resid, message)
    return correction, lin_residual, rms[0, 0]


def solution(mesh):
    placed = (P("gz", "gy", None),) * 4
    return jax.shard_map(
        shards,
        mesh=mesh,
        in_specs=placed,
        out_specs=(P("gz", "gy", None), P("gz", "gy", None), P()),
        check_vma=False,
    )
```

```python
import functools

import jax
import jax.numpy as jnp
import ml_dtypes
import numpy as np
from jax import lax
from jax.experimental import pallas as pl
from jax.experimental.pallas import tpu as pltpu
from jax.sharding import PartitionSpec as P

F32 = jnp.float32
BF16 = jnp.bfloat16
NZ, NY, NX = 512, 256, 128
GZ, GY = 32, 4
ZC, YC = NZ // GZ, NY // GY
FR = YC + 16
WIDE = FR + 16
WR, WC, RING = 23, 22, 3
LANES = 512
YP, XP = 4, 8
ROW0 = (0, 17, 33, 49)
VMEM_LIMIT = 40 * 1024 * 1024


def segments(block):
    found = [(WC * (row // 4), row) for row in range(block, WR, 4)]
    if block < 3:
        found = [(0, found[-1][1]), (RING - block, found[0][1])] + found[1:]
    return found


def window_places():
    place = np.full((8, LANES), -1000, np.int32)
    for block in range(4):
        parts = segments(block) + [(128, None)]
        for (begin, row), (end, _) in zip(parts[:-1], parts[1:]):
            for lane in range(begin, end):
                column = (lane - WC * (row // 4)) % 128
                if column < WC:
                    place[0, 128 * block + lane] = row
                    place[1, 128 * block + lane] = column
    return place


def tables():
    index = np.arange(NZ, dtype=np.int64)
    phase = (index[:, None] + 1) * (index[None, :] + 1) % (2 * (NZ + 1))
    table = np.sqrt(2.0 / (NZ + 1)) * np.sin(np.pi * phase / (NZ + 1))
    table = table.astype(np.float32)
    high = table.astype(ml_dtypes.bfloat16)
    low = (table - high.astype(np.float32)).astype(ml_dtypes.bfloat16)
    lam = 2.0 - 2.0 * np.cos(np.pi * (index + 1.0) / (NZ + 1))
    lam = np.broadcast_to(lam.astype(np.float32)[:, None], (NZ, 128))
    ahead_high, ahead_low = np.roll(high, 2, 1), np.roll(low, 2, 1)
    return ahead_high, ahead_low, high, low, np.ascontiguousarray(lam), window_places()


def lane_iota(shape):
    return lax.broadcasted_iota(jnp.int32, shape, len(shape) - 1)


def roll(value, shift, axis):
    return pltpu.roll(value, shift % value.shape[axis], axis)


def start_all(pairs, sems):
    copies = [pltpu.make_async_copy(x, y, sems.at[k]) for k, (x, y) in enumerate(pairs)]
    for copy in copies:
        copy.start()
    return copies


def behind_kernel(it, src, out, sems):
    for copy in start_all(
        ((it.at[ZC - 3:ZC], out.at[0:3]), (src.at[ZC - 2:ZC], out.at[3:5])), sems
    ):
        copy.wait()


def edge_kernel(it, src, reg, msk, up, down, it_out, src_out, reg_out, msk_out,
                e_it, e_src, e_reg, e_msk, sems):
    pairs = []
    for side, row in enumerate((0, YC - 8)):
        rows = pl.ds(row, 8)
        pairs += [
            (it.at[:, rows], e_it.at[side]),
            (src.at[:, rows], e_src.at[side]),
            (reg.at[0:1, rows], e_reg.at[side]),
            (msk.at[0:1, rows], e_msk.at[side]),
        ]
    pairs += [
        (it, it_out), (src.at[0:ZC - 2], src_out), (reg.at[0:1], reg_out), (msk.at[0:1], msk_out),
    ]
    copies = start_all(pairs, sems)
    for copy in copies[:-4]:
        copy.wait()
    for z in range(ZC):
        up[5 * z:5 * z + 5] = e_it[1, z, 3:8]
        down[6 * z:6 * z + 6] = e_it[0, z, 0:6]
    for z in range(ZC - 2):
        up[80 + 4 * z:84 + 4 * z] = e_src[1, z, 4:8]
        down[96 + 4 * z:100 + 4 * z] = e_src[0, z, 0:4]
    up[136:141] = e_reg[1, 0, 3:8].astype(F32)
    up[141:145] = e_msk[1, 0, 4:8].astype(F32)
    up[145:152] = jnp.zeros((7, 128), F32)
    down[152:157] = e_reg[0, 0, 0:5].astype(F32)
    down[157:161] = e_msk[0, 0, 0:4].astype(F32)
    down[161:168] = jnp.zeros((7, 128), F32)
    for copy in copies[-4:]:
        copy.wait()


def corner_kernel(zgot, up, down):
    for p in range(3):
        up[5 * p:5 * p + 5] = zgot[p, YC - 5:YC]
        down[6 * p:6 * p + 6] = zgot[p, 0:6]
    for q in range(2):
        up[15 + 4 * q:19 + 4 * q] = zgot[3 + q, YC - 4:YC]
        down[18 + 4 * q:22 + 4 * q] = zgot[3 + q, 0:4]
    up[23:24] = jnp.zeros((1, 128), F32)
    down[26:32] = jnp.zeros((6, 128), F32)


MID = slice(8, 8 + YC)


def edge_lanes():
    lane = lane_iota((FR, 128))
    return lane == 0, lane == 127


def level(frame, p, shift=0):
    return frame[p, 8 + shift:8 + shift + FR]


def set_nu(p, field, right, nu, iron, last):
    u, uz = level(field, p), level(field, p + 1)
    if p == 2:
        uz = jnp.where(lax.axis_index("gz") == 0, 0.0, uz)
    ux = jnp.where(last, 0.0, roll(u, -1, 1))
    right[p] = ux
    dz = uz - u
    dy = level(field, p, 1) - u
    dx = ux - u
    bsq = dz * dz + dy * dy + dx * dx
    bsq = bsq * bsq
    nu[p, 8:8 + FR] = jnp.where(iron, 0.05 + bsq / (bsq + 9.0), 1.0)


def set_residuals(count, field, right, nu, drive, flat, rows, resid, message, first, last):
    start = lax.axis_index("gz") == 0
    copper, held = flat[0] == 1.0, flat[1] == 1.0
    flux = 0.5 * (level(nu, 0) + level(nu, 1)) * (level(field, 0) - level(field, 1))
    for t in range(count):
        p = t + 1
        u, n = level(field, p), level(nu, p)
        uz, nz = level(field, p + 1), level(nu, p + 1)
        if p == 2:
            uz, nz = jnp.where(start, 0.0, uz), jnp.where(start, 1.0, nz)
        if p == 3:
            flux = jnp.where(start, -0.5 * (1.0 + n) * u, flux)
        ahead = 0.5 * (n + nz) * (u - uz)
        flow = ahead - flux
        flux = ahead
        flow = flow + 0.5 * (n + level(nu, p, 1)) * (u - level(field, p, 1))
        flow = flow + 0.5 * (n + level(nu, p, -1)) * (u - level(field, p, -1))
        nx = jnp.where(last, 1.0, roll(n, -1, 1))
        fx = 0.5 * (n + nx) * (u - right[p])
        flow = flow + (fx - jnp.where(first, -0.5 * (n + 1.0) * u, roll(fx, 1, 1)))
        value = -jnp.where(held, u, flow - jnp.where(copper, drive[t], 0.0))
        rows[t * FR:t * FR + FR, :] = value
        if t < 2:
            message[3 * FR + YC * t:3 * FR + YC * t + YC, :] = value[MID]
        else:
            resid[t - 2] = value[MID]


def set_means(total, rows, first, last):
    rows[16 * FR:17 * FR, :] = total
    rows[17 * FR:18 * FR, :] = 2.0 * total + 0.5 * (
        roll(total, -1, 0) + roll(total, 1, 0)
        + jnp.where(last, float(ZC), roll(total, -1, 1))
        + jnp.where(first, float(ZC), roll(total, 1, 1))
    )


def pack(rows, chunks, parts_y, tiles):
    lane = lane_iota((8, 128))
    places = [(lane - 16 * xp) & 127 for xp in range(XP)]
    for yp in parts_y:
        for block in range(4):
            parts = segments(block)
            turned = {}
            for begin, row in parts:
                at = ROW0[yp] + row + 4
                turned[row] = [
                    roll(
                        rows[pl.ds(8 * tile * FR + at, 8, stride=FR), :],
                        WC * (row // 4) + RING, 1,
                    )
                    for tile in tiles
                ]
            for xp in range(XP):
                values = turned[parts[0][1]]
                for begin, row in parts[1:]:
                    later = places[xp] >= begin
                    values = [jnp.where(later, x, y) for x, y in zip(turned[row], values)]
                peer, at = yp * XP + xp, 16 * block
                for tile, value in zip(tiles, values):
                    if tile < 2:
                        chunks[peer, at + 8 * tile:at + 8 * tile + 8, :] = value
                    else:
                        chunks[peer, 64 + 2 * block:66 + 2 * block, :] = value[0:2]


def residual_kernel(it, src, reg, msk, zgot, lo, hi,
                    chunks, nu, resid, message, rows, field, right, drive, flat, rest):
    column = lax.axis_index("gy")

    def below(value):
        return jnp.where(column == 0, 0.0, value)

    def above(value):
        return jnp.where(column == GY - 1, 0.0, value)

    for p in range(3):
        field[p, 16:16 + YC] = zgot[p]
    for z in range(ZC):
        field[z + 3, 16:16 + YC] = it[z]
        field[z + 3, 11:16] = below(lo[5 * z:5 * z + 5])
        field[z + 3, 80:86] = above(hi[6 * z:6 * z + 6])
    for t in range(2):
        drive[t, MID] = zgot[3 + t]
    for z in range(ZC - 2):
        drive[z + 2, MID] = src[z]
        drive[z + 2, 4:8] = lo[80 + 4 * z:84 + 4 * z]
        drive[z + 2, 72:76] = hi[96 + 4 * z:100 + 4 * z]
    flat[0, MID] = reg[0].astype(F32)
    flat[0, 3:8] = below(lo[136:141])
    flat[0, 72:77] = above(hi[152:157])
    flat[1, MID] = msk[0].astype(F32)
    flat[1, 4:8] = lo[141:145]
    flat[1, 72:76] = hi[157:161]
    first, last = edge_lanes()
    iron = flat[0] == 2.0
    for p in range(18):
        set_nu(p, field, right, nu, iron, last)
    total = level(nu, 3)
    for p in range(4, 17):
        total = total + level(nu, p)
    rest[...] = total
    for k in range(3):
        message[FR * k:FR * k + FR, :] = level(nu, 1 + k)
    set_residuals(ZC, field, right, nu, drive, flat, rows, resid, message, first, last)
    set_means(total + (level(nu, 1) + level(nu, 2)), rows, first, last)
    rows[18 * FR:24 * FR, :] = jnp.zeros((6 * FR, 128), F32)
    pack(rows, chunks, (1, 2), (0, 1, 2))
    pack(rows, chunks, (0, 3), (1,))


def corner_residual_kernel(corner_lo, corner_hi, flat, rest, *refs):
    chunks, nu, resid, message, rows, field, right, drive = refs[8:]
    column = lax.axis_index("gy")
    for p in range(3):
        field[p, 11:16] = jnp.where(column == 0, 0.0, corner_lo[5 * p:5 * p + 5])
        field[p, 80:86] = jnp.where(column == GY - 1, 0.0, corner_hi[6 * p:6 * p + 6])
    for t in range(2):
        drive[t, 4:8] = corner_lo[15 + 4 * t:19 + 4 * t]
        drive[t, 72:76] = corner_hi[18 + 4 * t:22 + 4 * t]
    first, last = edge_lanes()
    iron = flat[0] == 2.0
    for p in range(3):
        set_nu(p, field, right, nu, iron, last)
    for k in range(2):
        message[FR * k:FR * k + FR, :] = level(nu, 1 + k)
    set_residuals(3, field, right, nu, drive, flat, rows, resid, message, first, last)
    set_means(rest[...] + (level(nu, 1) + level(nu, 2)), rows, first, last)
    pack(rows, chunks, (0, 3), (0, 2))


def product(high, low, right_high, right_low):
    left = jnp.concatenate([high, low, high], axis=1)
    right = jnp.concatenate([right_high, right_high, right_low], axis=0)
    return jnp.dot(left, right, preferred_element_type=F32)


def modes_kernel(got, ahead_high, ahead_low, high, low, lam, spots, out, lines, back):
    group, column = lax.axis_index("gz"), lax.axis_index("gy")
    yp, xp = lax.div(group, XP), lax.rem(group, XP)
    s_high, s_low = ahead_high[...], ahead_low[...]
    for half in range(2):
        value = jnp.concatenate(
            [
                got[:, 16 * block:16 * block + 16, :].reshape(NZ, 128)
                for block in (2 * half, 2 * half + 1)
            ],
            axis=1,
        )
        v_high = value.astype(BF16)
        v_low = (value - v_high.astype(F32)).astype(BF16)
        lines[:, 256 * half:256 * half + 256] = product(s_high, s_low, v_high, v_low)

    sums = jnp.sum(got[:, 64:72, :], axis=0) * (1.0 / NZ)
    mean = [sums[2 * b:2 * b + 1] for b in range(4)]
    faces = [sums[2 * b + 1:2 * b + 2] for b in range(4)]
    turned = [pltpu.roll(spots[:, 128 * b:128 * b + 128], 16 * xp, 1) for b in range(4)]
    row = jnp.concatenate([place[0:1] for place in turned], axis=1)
    col = jnp.concatenate([place[1:2] for place in turned], axis=1)
    ypos = column * YC + 16 * yp + jnp.where(yp > 0, 1, 0) + row - 4
    xpos = 16 * xp - RING + col
    inside = (row >= 0) & (xpos >= 0) & (xpos < NX) & (ypos >= 0) & (ypos < NY)
    right = [0.5 * (m + roll(m, -1, 1)) for m in mean]
    left = [roll(r, 1, 1) for r in right]
    above = [0.5 * (mean[b] + mean[b + 1]) for b in range(3)]
    above.append(0.5 * (mean[3] + roll(mean[0], -WC, 1)))
    below = [roll(above[3], WC, 1)] + above[:3]

    lam_rows = lam[...]
    vhat = [lines[:, 128 * b:128 * b + 128] for b in range(4)]
    factor = [
        jnp.where(inside[:, 128 * b:128 * b + 128], 0.6 / (faces[b] + lam_rows * mean[b]), 0.0)
        for b in range(4)
    ]
    w = [factor[b] * vhat[b] for b in range(4)]
    for _ in range(3):
        after = w[1:] + [roll(w[0], -WC, 1)]
        before = [roll(w[3], WC, 1)] + w[:3]
        near = [
            above[b] * after[b] + below[b] * before[b]
            + right[b] * roll(w[b], -1, 1) + left[b] * roll(w[b], 1, 1)
            for b in range(4)
        ]
        w = [0.4 * w[b] + factor[b] * (vhat[b] + near[b]) for b in range(4)]
    w = jnp.concatenate(w, axis=1)
    w_high = w.astype(BF16)
    w_low = (w - w_high.astype(F32)).astype(BF16)

    spot = lane_iota((LANES, 384))
    own = jnp.where(yp == 0, 1, 0)
    halo = jnp.where(yp == 0, 0, 16)
    inner = (spot - 16 * xp) & 127
    line = RING + jnp.where(spot < 256, own + 8 * (spot >> 7) + (inner >> 4), halo)
    pick = 128 * (line & 3) + ((WC * (line >> 2) + RING + (spot & 15) + 16 * xp) & 127)
    choose = jnp.where(lax.broadcasted_iota(jnp.int32, (LANES, 384), 0) == pick, 1.0, 0.0)
    choose = choose.astype(BF16)
    s_high, s_low = high[...], low[...]
    w_high = jnp.dot(w_high, choose, preferred_element_type=F32).astype(BF16)
    w_low = jnp.dot(w_low, choose, preferred_element_type=F32).astype(BF16)
    back[8:8 + NZ, :] = product(s_high, s_low, w_high, w_low)
    back[0:8, :] = jnp.zeros((8, 384), F32)
    back[8 + NZ:, :] = jnp.zeros((8, 384), F32)

    sub = lax.broadcasted_iota(jnp.int32, (8, 128), 0)
    pattern = (((lane_iota((8, 128)) >> 4) + sub - xp) & 7) == 0
    for peer in range(GZ):
        at = 8 + ZC * peer
        for block in range(2):
            lanes = slice(128 * block, 128 * block + 128)
            out[peer, 16 * block:16 * block + 16, :] = back[at:at + ZC, lanes]
            out[peer, 32 + block:33 + block, :] = back[at - 1:at, lanes]
            out[peer, 34 + block:35 + block, :] = back[at + ZC:at + ZC + 1, lanes]
            piece = back[at + 8 * block:at + 8 * block + 8, 256:384]
            piece = jnp.sum(jnp.where(pattern, piece, 0.0), axis=0, keepdims=True)
            out[peer, 36 + block:37 + block, :] = piece
        out[peer, 38:40, :] = jnp.zeros((2, 128), F32)


def resid_plane(resid, message, z):
    if z < ZC - 2:
        return resid[z]
    at = 3 * FR + YC * (z - ZC + 2)
    return message[at:at + YC, :]


def image_kernel(got, nu, resid, message, msk, zdir, image, sums, frame):
    lane = lane_iota((8, 128))
    places = [(lane >> 4) == k for k in range(8)]

    def spread(tiles, jj):
        value = tiles[0]
        for xp in range(1, XP):
            value = jnp.where(places[(jj + xp) % 8], tiles[xp], value)
        return roll(value, -16 * jj, 1)

    for yp in range(YP):
        for block in range(2):
            for tile in range(2):
                at = 16 * block + 8 * tile
                tiles = [got[yp * XP + xp, at:at + 8, :] for xp in range(XP)]
                for jj in range(8):
                    y = 8 + 16 * yp + 8 * block + jj
                    frame[pl.ds((1 + 8 * tile) * FR + y, 8, stride=FR), :] = spread(tiles, jj)
        tiles = [got[yp * XP + xp, 32:40, :] for xp in range(XP)]
        for jj in range(8):
            value = spread(tiles, jj)
            y = 8 + 16 * yp + jj
            for k in range(2):
                frame[y + 8 * k:y + 8 * k + 1, :] = value[k:k + 1]
                at = 17 * FR + y + 8 * k
                frame[at:at + 1, :] = value[2 + k:3 + k]

    sub = lax.broadcasted_iota(jnp.int32, (8, 128), 0)
    turn = ((lane >> 4) + sub) & 7
    for yp, y in ((0, 7), (YP - 1, 8 + YC)):
        for tile in range(2):
            value = jnp.zeros((8, 128), F32)
            for xp in range(XP):
                line = got[yp * XP + xp, 36 + tile:37 + tile, :]
                value = jnp.where(turn == xp, jnp.broadcast_to(line, (8, 128)), value)
            value = pltpu.roll(value, 0, 1, stride=16, stride_axis=0)
            frame[pl.ds((1 + 8 * tile) * FR + y, 8, stride=FR), :] = value

    lane = lane_iota((YC, 128))
    first, last = lane == 0, lane == 127
    held = msk[0] == 1

    group = lax.axis_index("gz")

    def nu_rows(z, shift):
        at = 8 + shift
        if z >= ZC - 2:
            value = message[FR * (z - ZC + 2) + at:FR * (z - ZC + 2) + at + YC, :]
        else:
            value = nu[z + 3, at + 8:at + 8 + YC]
        if z == -1:
            value = jnp.where(group == 0, 1.0, value)
        if z == ZC:
            value = jnp.where(group == GZ - 1, 1.0, value)
        return value

    def dir_rows(z, shift):
        at = (z + 1) * FR + 8 + shift
        return frame[at:at + YC, :]

    d, n = dir_rows(0, 0), nu_rows(0, 0)
    flux = 0.5 * (nu_rows(-1, 0) + n) * (dir_rows(-1, 0) - d)
    rr = ri = ii = jnp.zeros((8, 128), F32)

    def fold(value):
        return jnp.sum(value.reshape(YC // 8, 8, 128), axis=0)

    for z in range(ZC):
        dz, nz = dir_rows(z + 1, 0), nu_rows(z + 1, 0)
        ahead = 0.5 * (n + nz) * (d - dz)
        flow = ahead - flux
        flow = flow + 0.5 * (n + nu_rows(z, 1)) * (d - dir_rows(z, 1))
        flow = flow + 0.5 * (n + nu_rows(z, -1)) * (d - dir_rows(z, -1))
        nx = jnp.where(last, 1.0, roll(n, -1, 1))
        dx = jnp.where(last, 0.0, roll(d, -1, 1))
        fx = 0.5 * (n + nx) * (d - dx)
        flow = flow + (fx - jnp.where(first, -0.5 * (n + 1.0) * d, roll(fx, 1, 1)))
        value = jnp.where(held, d, flow)
        zdir[z] = d
        image[z] = value
        r = resid_plane(resid, message, z)
        rr, ri, ii = rr + fold(r * r), ri + fold(r * value), ii + fold(value * value)
        d, n, flux = dz, nz, ahead

    parts = (rr, ri, ii)
    line = lane_iota((1, 128))
    packed = jnp.zeros((1, 128), F32)
    for k, part in enumerate(parts):
        packed = jnp.where(line == k, jnp.sum(part), packed)
    sums[...] = jnp.broadcast_to(packed[None], sums.shape)


def output_kernel(sums, zdir, image, resid, message, correction, lin_residual, rms):
    total = jnp.sum(sums[...], axis=0)
    beta_sq = total[0:1, 0:1] + 1e-06
    beta = jnp.sqrt(beta_sq)
    h_one = total[0:1, 1:2] / beta_sq
    denom = total[0:1, 2:3] / beta_sq - h_one * h_one * (1e-06 / beta_sq) + 1e-06
    gamma = h_one / denom
    correction[...] = zdir[...] * gamma[None]
    for z in range(ZC):
        lin_residual[z] = resid_plane(resid, message, z) - gamma * image[z]
    rms[...] = jnp.broadcast_to(beta * (1.0 / np.sqrt(float(NZ * NY * NX))), rms.shape)


def call(kernel, out_shape, scratch=(), **extra):
    return pl.pallas_call(
        kernel,
        out_shape=out_shape,
        scratch_shapes=scratch,
        compiler_params=pltpu.CompilerParams(vmem_limit_bytes=VMEM_LIMIT),
        **extra,
    )


def struct(*shape):
    return jax.ShapeDtypeStruct(shape, F32)


def cyclic(count, step):
    return [(i, (i + step) % count) for i in range(count)]


def shards(iterate, source, region, fixed_mask):
    far = pl.BlockSpec(memory_space=pltpu.HBM)
    cells = (ZC, YC, 128)
    arguments = [
        pltpu.with_memory_space_constraint(argument, pltpu.HBM)
        for argument in (iterate, source, region, fixed_mask)
    ]
    edge = (2, ZC, 8, 128)
    flat = jax.ShapeDtypeStruct((1, YC, 128), jnp.int32)
    zmsg = call(
        behind_kernel, struct(5, YC, 128),
        scratch=[pltpu.SemaphoreType.DMA((2,))], in_specs=[far] * 2,
    )(*arguments[:2])
    zgot = lax.ppermute(zmsg, "gz", cyclic(GZ, 1))
    up, down, it, src, reg, msk = call(
        edge_kernel,
        (
            struct(152, 128), struct(168, 128),
            struct(*cells), struct(ZC - 2, YC, 128), flat, flat,
        ),
        scratch=[
            pltpu.VMEM(edge, F32), pltpu.VMEM(edge, F32),
            pltpu.VMEM((2, 1, 8, 128), jnp.int32), pltpu.VMEM((2, 1, 8, 128), jnp.int32),
            pltpu.SemaphoreType.DMA((12,)),
        ],
        in_specs=[far] * 4,
    )(*arguments)
    lo = lax.ppermute(up, "gy", cyclic(GY, 1))
    hi = lax.ppermute(down, "gy", cyclic(GY, -1))
    corner_up, corner_down = call(corner_kernel, (struct(24, 128), struct(32, 128)))(zgot)
    corner_lo = lax.ppermute(corner_up, "gy", cyclic(GY, 1))
    corner_hi = lax.ppermute(corner_down, "gy", cyclic(GY, -1))

    kept = (
        struct(GZ, 72, 128), struct(18, WIDE, 128), struct(ZC - 2, YC, 128),
        struct(3 * FR + 2 * YC, 128), struct(24 * FR, 128), struct(19, WIDE, 128),
        struct(18, FR, 128), struct(ZC, FR, 128),
    )
    *early, frames, rest = call(
        residual_kernel, kept + (struct(2, FR, 128), struct(FR, 128))
    )(it, src, reg, msk, zgot, lo, hi)
    chunks, nu, resid, message, *_ = call(
        corner_residual_kernel, kept, input_output_aliases={4 + k: k for k in range(len(kept))}
    )(corner_lo, corner_hi, frames, rest, *early)
    message = lax.ppermute(message, "gz", cyclic(GZ, -1))
    windows = lax.all_to_all(chunks, "gz", 0, 0, tiled=True)
    sent = call(
        modes_kernel,
        struct(GZ, 40, 128),
        scratch=[
            pltpu.VMEM((NZ, LANES), F32), pltpu.VMEM((NZ + 16, 384), F32),
        ],
    )(windows, *[jnp.asarray(table) for table in tables()])
    returned = lax.all_to_all(sent, "gz", 0, 0, tiled=True)
    zdir, image, sums = call(
        image_kernel,
        (struct(*cells), struct(*cells), struct(GZ * GY, 1, 128)),
        scratch=[pltpu.VMEM((18 * FR, 128), F32)],
    )(returned, nu, resid, message, msk)
    sums = lax.all_to_all(sums, ("gz", "gy"), 0, 0, tiled=True)
    correction, lin_residual, rms = call(
        output_kernel, (struct(*cells), struct(*cells), struct(1, 128))
    )(sums, zdir, image, resid, message)
    return correction, lin_residual, rms[0, 0]


def solution(mesh):
    placed = (P("gz", "gy", None),) * 4
    return jax.shard_map(
        shards,
        mesh=mesh,
        in_specs=placed,
        out_specs=(P("gz", "gy", None), P("gz", "gy", None), P()),
        check_vma=False,
    )
```

```python
import functools

import jax
import jax.numpy as jnp
import ml_dtypes
import numpy as np
from jax import lax
from jax.experimental import pallas as pl
from jax.experimental.pallas import tpu as pltpu
from jax.sharding import PartitionSpec as P

F32 = jnp.float32
BF16 = jnp.bfloat16
NZ, NY, NX = 512, 256, 128
GZ, GY = 32, 4
ZC, YC = NZ // GZ, NY // GY
FR = YC + 16
WIDE = FR + 16
WR, WC, RING = 23, 22, 3
LANES = 512
YP, XP = 4, 8
ROW0 = (0, 17, 33, 49)
VMEM_LIMIT = 40 * 1024 * 1024
COST = pl.CostEstimate(flops=4_000_000, bytes_accessed=8_000_000, transcendentals=0)


def segments(block):
    found = [(WC * (row // 4), row) for row in range(block, WR, 4)]
    if block < 3:
        found = [(0, found[-1][1]), (RING - block, found[0][1])] + found[1:]
    return found


def window_places():
    place = np.full((8, LANES), -1000, np.int32)
    for block in range(4):
        parts = segments(block) + [(128, None)]
        for (begin, row), (end, _) in zip(parts[:-1], parts[1:]):
            for lane in range(begin, end):
                column = (lane - WC * (row // 4)) % 128
                if column < WC:
                    place[0, 128 * block + lane] = row
                    place[1, 128 * block + lane] = column
    return place


def tables():
    index = np.arange(NZ, dtype=np.int64)
    phase = (index[:, None] + 1) * (index[None, :] + 1) % (2 * (NZ + 1))
    table = np.sqrt(2.0 / (NZ + 1)) * np.sin(np.pi * phase / (NZ + 1))
    table = table.astype(np.float32)
    high = table.astype(ml_dtypes.bfloat16)
    low = (table - high.astype(np.float32)).astype(ml_dtypes.bfloat16)
    lam = 2.0 - 2.0 * np.cos(np.pi * (index + 1.0) / (NZ + 1))
    lam = np.broadcast_to(lam.astype(np.float32)[:, None], (NZ, 128))
    ahead_high, ahead_low = np.roll(high, 2, 1), np.roll(low, 2, 1)
    return ahead_high, ahead_low, high, low, np.ascontiguousarray(lam), window_places()


def lane_iota(shape):
    return lax.broadcasted_iota(jnp.int32, shape, len(shape) - 1)


def roll(value, shift, axis):
    return pltpu.roll(value, shift % value.shape[axis], axis)


def start_all(pairs, sems):
    copies = [pltpu.make_async_copy(x, y, sems.at[k]) for k, (x, y) in enumerate(pairs)]
    for copy in copies:
        copy.start()
    return copies


def edge_kernel(it, src, reg, msk, zmsg, up, down, e_it, e_src, e_reg, e_msk, sems):
    pairs = [(it.at[ZC - 3:ZC], zmsg.at[0:3]), (src.at[ZC - 2:ZC], zmsg.at[3:5])]
    for side, row in enumerate((0, YC - 8)):
        rows = pl.ds(row, 8)
        pairs += [
            (it.at[:, rows], e_it.at[side]),
            (src.at[:, rows], e_src.at[side]),
            (reg.at[0:1, rows], e_reg.at[side]),
            (msk.at[0:1, rows], e_msk.at[side]),
        ]
    copies = start_all(pairs, sems)
    for copy in copies[2:]:
        copy.wait()
    for z in range(ZC):
        up[5 * z:5 * z + 5] = e_it[1, z, 3:8]
        down[6 * z:6 * z + 6] = e_it[0, z, 0:6]
        up[80 + 4 * z:84 + 4 * z] = e_src[1, z, 4:8]
        down[96 + 4 * z:100 + 4 * z] = e_src[0, z, 0:4]
    up[144:149] = e_reg[1, 0, 3:8].astype(F32)
    up[149:153] = e_msk[1, 0, 4:8].astype(F32)
    up[153:160] = jnp.zeros((7, 128), F32)
    down[160:165] = e_reg[0, 0, 0:5].astype(F32)
    down[165:169] = e_msk[0, 0, 0:4].astype(F32)
    down[169:176] = jnp.zeros((7, 128), F32)
    for copy in copies[:2]:
        copy.wait()


def corner_kernel(lo, hi, out):
    out[0:15] = lo[65:80]
    out[15:33] = hi[78:96]
    out[33:41] = lo[136:144]
    out[41:49] = hi[152:160]
    out[49:56] = jnp.zeros((7, 128), F32)


INNER, OUTER = ((8, YC),), ((0, 16), (YC, 16))


def edge_lanes(count):
    lane = lane_iota((count, 128))
    return lane == 0, lane == 127


def level(frame, p, span, shift=0):
    return frame[p, pl.ds(8 + span[0] + shift, span[1])]


def set_nu(p, span, field, right, nu, iron, last):
    u, uz = level(field, p, span), level(field, p + 1, span)
    if p == 2:
        uz = jnp.where(lax.axis_index("gz") == 0, 0.0, uz)
    ux = jnp.where(last, 0.0, roll(u, -1, 1))
    right[p, pl.ds(*span)] = ux
    dz = uz - u
    dy = level(field, p, span, 1) - u
    dx = ux - u
    bsq = dz * dz + dy * dy + dx * dx
    bsq = bsq * bsq
    nu[p, pl.ds(8 + span[0], span[1])] = jnp.where(iron, 0.05 + bsq / (bsq + 9.0), 1.0)


def set_residuals(span, steps, field, right, nu, drive, flat, rows, resid, message, first, last):
    start = lax.axis_index("gz") == 0
    begin, count = span
    copper, held = flat[0, pl.ds(*span)] == 1.0, flat[1, pl.ds(*span)] == 1.0
    own = max(begin, 8)
    own = slice(own - begin, min(begin + count, 8 + YC) - begin)
    kept = pl.ds(begin + own.start - 8, own.stop - own.start)
    p = steps[0]
    flux = 0.5 * (level(nu, p, span) + level(nu, p + 1, span)) * (
        level(field, p, span) - level(field, p + 1, span)
    )
    for t in steps:
        p = t + 1
        u, n = level(field, p, span), level(nu, p, span)
        uz, nz = level(field, p + 1, span), level(nu, p + 1, span)
        if p == 2:
            uz, nz = jnp.where(start, 0.0, uz), jnp.where(start, 1.0, nz)
        if p == 3:
            flux = jnp.where(start, -0.5 * (1.0 + n) * u, flux)
        ahead = 0.5 * (n + nz) * (u - uz)
        flow = ahead - flux
        flux = ahead
        flow = flow + 0.5 * (n + level(nu, p, span, 1)) * (u - level(field, p, span, 1))
        flow = flow + 0.5 * (n + level(nu, p, span, -1)) * (u - level(field, p, span, -1))
        nx = jnp.where(last, 1.0, roll(n, -1, 1))
        fx = 0.5 * (n + nx) * (u - right[p, pl.ds(*span)])
        flow = flow + (fx - jnp.where(first, -0.5 * (n + 1.0) * u, roll(fx, 1, 1)))
        value = -jnp.where(held, u, flow - jnp.where(copper, drive[t, pl.ds(*span)], 0.0))
        rows[pl.ds(t * FR + begin, count), :] = value
        if t < 2:
            message[pl.ds(3 * FR + YC * t + kept.start, kept.size), :] = value[own]
        else:
            resid[t - 2, kept] = value[own]


def set_means(span, rows, first, last):
    begin, count = 16 * FR + span[0], span[1]
    total = rows[pl.ds(begin, count), :]
    rows[pl.ds(begin + FR, count), :] = 2.0 * total + 0.5 * (
        rows[pl.ds(begin - 1, count), :] + rows[pl.ds(begin + 1, count), :]
        + jnp.where(last, float(ZC), roll(total, -1, 1))
        + jnp.where(first, float(ZC), roll(total, 1, 1))
    )


def work(spans, planes, steps, field, right, nu, drive, flat, rows, resid, message):
    for span in spans:
        first, last = edge_lanes(span[1])
        iron = flat[0, pl.ds(*span)] == 2.0
        for p in planes:
            set_nu(p, span, field, right, nu, iron, last)
        for p in planes:
            if 1 <= p < 4:
                message[pl.ds(FR * (p - 1) + span[0], span[1]), :] = level(nu, p, span)
    for span in spans:
        first, last = edge_lanes(span[1])
        set_residuals(
            span, steps, field, right, nu, drive, flat, rows, resid, message, first, last
        )


def sum_planes(spans, nu, rows):
    for span in spans:
        total = level(nu, 1, span)
        for p in range(2, 17):
            total = total + level(nu, p, span)
        rows[pl.ds(16 * FR + span[0], span[1]), :] = total
    for span in spans:
        set_means(span, rows, *edge_lanes(span[1]))


def pack(rows, chunks, parts_y, tiles):
    lane = lane_iota((8, 128))
    places = [(lane - 16 * xp) & 127 for xp in range(XP)]
    for yp in parts_y:
        for block in range(4):
            parts = segments(block)
            turned = {}
            for begin, row in parts:
                at = ROW0[yp] + row + 4
                turned[row] = [
                    roll(
                        rows[pl.ds(8 * tile * FR + at, 8, stride=FR), :],
                        WC * (row // 4) + RING, 1,
                    )
                    for tile in tiles
                ]
            for xp in range(XP):
                values = turned[parts[0][1]]
                for begin, row in parts[1:]:
                    later = places[xp] >= begin
                    values = [jnp.where(later, x, y) for x, y in zip(turned[row], values)]
                peer, at = yp * XP + xp, 16 * block
                for tile, value in zip(tiles, values):
                    if tile < 2:
                        chunks[peer, at + 8 * tile:at + 8 * tile + 8, :] = value
                    else:
                        chunks[peer, 64 + 2 * block:66 + 2 * block, :] = value[0:2]


BEHIND, HERE = range(0, 3), range(3, 18)


def inner_kernel(it, src, reg, msk, chunks, nu, resid, message, rows, field, right, drive, flat,
                 reg_in, msk_in, sems):
    own = slice(8, 8 + YC)
    copies = start_all(
        (
            (it, field.at[3:19, 16:16 + YC]), (src.at[0:ZC - 2], drive.at[2:ZC, own]),
            (reg.at[0:1], reg_in), (msk.at[0:1], msk_in),
        ),
        sems,
    )
    rows[18 * FR:24 * FR, :] = jnp.zeros((6 * FR, 128), F32)
    for copy in copies:
        copy.wait()
    flat[0, own] = reg_in[0].astype(F32)
    flat[1, own] = msk_in[0].astype(F32)
    work(INNER, HERE, range(3, ZC), field, right, nu, drive, flat, rows, resid, message)
    pack(rows, chunks, (1, 2), (1,))


def halo_kernel(zgot, lo, hi, *refs):
    chunks, nu, resid, message, rows, field, right, drive, flat = refs[9:]
    column = lax.axis_index("gy")

    def below(value):
        return jnp.where(column == 0, 0.0, value)

    def above(value):
        return jnp.where(column == GY - 1, 0.0, value)

    for p in range(3):
        field[p, 16:16 + YC] = zgot[p]
    for z in range(ZC):
        field[z + 3, 11:16] = below(lo[5 * z:5 * z + 5])
        field[z + 3, 80:86] = above(hi[6 * z:6 * z + 6])
    for t in range(2):
        drive[t, 8:8 + YC] = zgot[3 + t]
    for z in range(ZC - 2):
        drive[z + 2, 4:8] = lo[80 + 4 * z:84 + 4 * z]
        drive[z + 2, 72:76] = hi[96 + 4 * z:100 + 4 * z]
    flat[0, 3:8] = below(lo[144:149])
    flat[0, 72:77] = above(hi[160:165])
    flat[1, 4:8] = lo[149:153]
    flat[1, 72:76] = hi[165:169]
    work(INNER, BEHIND, range(0, 3), field, right, nu, drive, flat, rows, resid, message)
    work(OUTER, HERE, range(3, ZC), field, right, nu, drive, flat, rows, resid, message)
    sum_planes(INNER, nu, rows)
    pack(rows, chunks, (1, 2), (0, 2))
    pack(rows, chunks, (0, 3), (1,))


def corner_residual_kernel(corners, *refs):
    chunks, nu, resid, message, rows, field, right, drive, flat = refs[9:]
    column = lax.axis_index("gy")
    for p in range(3):
        field[p, 11:16] = jnp.where(column == 0, 0.0, corners[5 * p:5 * p + 5])
        field[p, 80:86] = jnp.where(column == GY - 1, 0.0, corners[15 + 6 * p:21 + 6 * p])
    for t in range(2):
        drive[t, 4:8] = corners[33 + 4 * t:37 + 4 * t]
        drive[t, 72:76] = corners[41 + 4 * t:45 + 4 * t]
    work(OUTER, BEHIND, range(0, 3), field, right, nu, drive, flat, rows, resid, message)
    sum_planes(OUTER, nu, rows)
    pack(rows, chunks, (0, 3), (0, 2))


def product(high, low, right_high, right_low):
    left = jnp.concatenate([high, low, high], axis=1)
    right = jnp.concatenate([right_high, right_high, right_low], axis=0)
    return jnp.dot(left, right, preferred_element_type=F32)


def modes_kernel(got, ahead_high, ahead_low, high, low, lam, spots, out, lines, back):
    group, column = lax.axis_index("gz"), lax.axis_index("gy")
    yp, xp = lax.div(group, XP), lax.rem(group, XP)
    s_high, s_low = ahead_high[...], ahead_low[...]
    for half in range(2):
        value = jnp.concatenate(
            [
                got[:, 16 * block:16 * block + 16, :].reshape(NZ, 128)
                for block in (2 * half, 2 * half + 1)
            ],
            axis=1,
        )
        v_high = value.astype(BF16)
        v_low = (value - v_high.astype(F32)).astype(BF16)
        lines[:, 256 * half:256 * half + 256] = product(s_high, s_low, v_high, v_low)

    sums = jnp.sum(got[:, 64:72, :], axis=0) * (1.0 / NZ)
    mean = [sums[2 * b:2 * b + 1] for b in range(4)]
    faces = [sums[2 * b + 1:2 * b + 2] for b in range(4)]
    turned = [pltpu.roll(spots[:, 128 * b:128 * b + 128], 16 * xp, 1) for b in range(4)]
    row = jnp.concatenate([place[0:1] for place in turned], axis=1)
    col = jnp.concatenate([place[1:2] for place in turned], axis=1)
    ypos = column * YC + 16 * yp + jnp.where(yp > 0, 1, 0) + row - 4
    xpos = 16 * xp - RING + col
    inside = (row >= 0) & (xpos >= 0) & (xpos < NX) & (ypos >= 0) & (ypos < NY)
    right = [0.5 * (m + roll(m, -1, 1)) for m in mean]
    left = [roll(r, 1, 1) for r in right]
    above = [0.5 * (mean[b] + mean[b + 1]) for b in range(3)]
    above.append(0.5 * (mean[3] + roll(mean[0], -WC, 1)))
    below = [roll(above[3], WC, 1)] + above[:3]

    spot = lane_iota((LANES, 384))
    own = jnp.where(yp == 0, 1, 0)
    halo = jnp.where(yp == 0, 0, 16)
    inner = (spot - 16 * xp) & 127
    line = RING + jnp.where(spot < 256, own + 8 * (spot >> 7) + (inner >> 4), halo)
    pick = 128 * (line & 3) + ((WC * (line >> 2) + RING + (spot & 15) + 16 * xp) & 127)
    choose = jnp.where(lax.broadcasted_iota(jnp.int32, (LANES, 384), 0) == pick, 1.0, 0.0)
    choose = choose.astype(BF16)
    s_high, s_low = high[...], low[...]
    total = None
    for start in range(0, NZ, 128):
        part = slice(start, start + 128)
        lam_rows = lam[part, :]
        vhat = [lines[part, 128 * b:128 * b + 128] for b in range(4)]
        factor = [
            jnp.where(inside[:, 128 * b:128 * b + 128], 0.6 / (faces[b] + lam_rows * mean[b]), 0.0)
            for b in range(4)
        ]
        w = [factor[b] * vhat[b] for b in range(4)]
        for _ in range(3):
            after = w[1:] + [roll(w[0], -WC, 1)]
            before = [roll(w[3], WC, 1)] + w[:3]
            near = [
                above[b] * after[b] + below[b] * before[b]
                + right[b] * roll(w[b], -1, 1) + left[b] * roll(w[b], 1, 1)
                for b in range(4)
            ]
            w = [0.4 * w[b] + factor[b] * (vhat[b] + near[b]) for b in range(4)]
        w = jnp.concatenate(w, axis=1)
        w_high = w.astype(BF16)
        w_low = (w - w_high.astype(F32)).astype(BF16)
        w_high = jnp.dot(w_high, choose, preferred_element_type=F32).astype(BF16)
        w_low = jnp.dot(w_low, choose, preferred_element_type=F32).astype(BF16)
        term = product(high[:, part], low[:, part], w_high, w_low)
        total = term if total is None else total + term
    back[8:8 + NZ, :] = total
    back[0:8, :] = jnp.zeros((8, 384), F32)
    back[8 + NZ:, :] = jnp.zeros((8, 384), F32)

    sub = lax.broadcasted_iota(jnp.int32, (8, 128), 0)
    pattern = (((lane_iota((8, 128)) >> 4) + sub - xp) & 7) == 0
    for peer in range(GZ):
        at = 8 + ZC * peer
        for block in range(2):
            lanes = slice(128 * block, 128 * block + 128)
            out[peer, 16 * block:16 * block + 16, :] = back[at:at + ZC, lanes]
            out[peer, 32 + block:33 + block, :] = back[at - 1:at, lanes]
            out[peer, 34 + block:35 + block, :] = back[at + ZC:at + ZC + 1, lanes]
            piece = back[at + 8 * block:at + 8 * block + 8, 256:384]
            piece = jnp.sum(jnp.where(pattern, piece, 0.0), axis=0, keepdims=True)
            out[peer, 36 + block:37 + block, :] = piece
        out[peer, 38:40, :] = jnp.zeros((2, 128), F32)


def resid_plane(resid, message, z):
    if z < ZC - 2:
        return resid[z]
    at = 3 * FR + YC * (z - ZC + 2)
    return message[at:at + YC, :]


def image_kernel(got, nu, resid, message, flat, zdir, image, sums, frame):
    lane = lane_iota((8, 128))
    places = [(lane >> 4) == k for k in range(8)]

    def spread(tiles, jj):
        value = tiles[0]
        for xp in range(1, XP):
            value = jnp.where(places[(jj + xp) % 8], tiles[xp], value)
        return roll(value, -16 * jj, 1)

    for yp in range(YP):
        for block in range(2):
            for tile in range(2):
                at = 16 * block + 8 * tile
                tiles = [got[yp * XP + xp, at:at + 8, :] for xp in range(XP)]
                for jj in range(8):
                    y = 8 + 16 * yp + 8 * block + jj
                    frame[pl.ds((1 + 8 * tile) * FR + y, 8, stride=FR), :] = spread(tiles, jj)
        tiles = [got[yp * XP + xp, 32:40, :] for xp in range(XP)]
        for jj in range(8):
            value = spread(tiles, jj)
            y = 8 + 16 * yp + jj
            for k in range(2):
                frame[y + 8 * k:y + 8 * k + 1, :] = value[k:k + 1]
                at = 17 * FR + y + 8 * k
                frame[at:at + 1, :] = value[2 + k:3 + k]

    sub = lax.broadcasted_iota(jnp.int32, (8, 128), 0)
    turn = ((lane >> 4) + sub) & 7
    for yp, y in ((0, 7), (YP - 1, 8 + YC)):
        for tile in range(2):
            value = jnp.zeros((8, 128), F32)
            for xp in range(XP):
                line = got[yp * XP + xp, 36 + tile:37 + tile, :]
                value = jnp.where(turn == xp, jnp.broadcast_to(line, (8, 128)), value)
            value = pltpu.roll(value, 0, 1, stride=16, stride_axis=0)
            frame[pl.ds((1 + 8 * tile) * FR + y, 8, stride=FR), :] = value

    lane = lane_iota((YC, 128))
    first, last = lane == 0, lane == 127
    held = flat[1, 8:8 + YC] == 1.0

    group = lax.axis_index("gz")

    def nu_rows(z, shift):
        at = 8 + shift
        if z >= ZC - 2:
            value = message[FR * (z - ZC + 2) + at:FR * (z - ZC + 2) + at + YC, :]
        else:
            value = nu[z + 3, at + 8:at + 8 + YC]
        if z == -1:
            value = jnp.where(group == 0, 1.0, value)
        if z == ZC:
            value = jnp.where(group == GZ - 1, 1.0, value)
        return value

    def dir_rows(z, shift):
        at = (z + 1) * FR + 8 + shift
        return frame[at:at + YC, :]

    d, n = dir_rows(0, 0), nu_rows(0, 0)
    flux = 0.5 * (nu_rows(-1, 0) + n) * (dir_rows(-1, 0) - d)
    rr = ri = ii = jnp.zeros((8, 128), F32)

    def fold(value):
        return jnp.sum(value.reshape(YC // 8, 8, 128), axis=0)

    for z in range(ZC):
        dz, nz = dir_rows(z + 1, 0), nu_rows(z + 1, 0)
        ahead = 0.5 * (n + nz) * (d - dz)
        flow = ahead - flux
        flow = flow + 0.5 * (n + nu_rows(z, 1)) * (d - dir_rows(z, 1))
        flow = flow + 0.5 * (n + nu_rows(z, -1)) * (d - dir_rows(z, -1))
        nx = jnp.where(last, 1.0, roll(n, -1, 1))
        dx = jnp.where(last, 0.0, roll(d, -1, 1))
        fx = 0.5 * (n + nx) * (d - dx)
        flow = flow + (fx - jnp.where(first, -0.5 * (n + 1.0) * d, roll(fx, 1, 1)))
        value = jnp.where(held, d, flow)
        zdir[z] = d
        image[z] = value
        r = resid_plane(resid, message, z)
        rr, ri, ii = rr + fold(r * r), ri + fold(r * value), ii + fold(value * value)
        d, n, flux = dz, nz, ahead

    parts = (rr, ri, ii)
    line = lane_iota((1, 128))
    packed = jnp.zeros((1, 128), F32)
    for k, part in enumerate(parts):
        packed = jnp.where(line == k, jnp.sum(part), packed)
    sums[...] = jnp.broadcast_to(packed[None], sums.shape)


def output_kernel(sums, zdir, image, resid, message, correction, lin_residual, rms):
    total = jnp.sum(sums[...], axis=0)
    beta_sq = total[0:1, 0:1] + 1e-06
    beta = jnp.sqrt(beta_sq)
    h_one = total[0:1, 1:2] / beta_sq
    denom = total[0:1, 2:3] / beta_sq - h_one * h_one * (1e-06 / beta_sq) + 1e-06
    gamma = h_one / denom
    correction[...] = zdir[...] * gamma[None]
    for z in range(ZC):
        lin_residual[z] = resid_plane(resid, message, z) - gamma * image[z]
    rms[...] = jnp.broadcast_to(beta * (1.0 / np.sqrt(float(NZ * NY * NX))), rms.shape)


def call(kernel, out_shape, scratch=(), **extra):
    return pl.pallas_call(
        kernel,
        out_shape=out_shape,
        scratch_shapes=scratch,
        compiler_params=pltpu.CompilerParams(vmem_limit_bytes=VMEM_LIMIT),
        **extra,
    )


def struct(*shape):
    return jax.ShapeDtypeStruct(shape, F32)


def cyclic(count, step):
    return [(i, (i + step) % count) for i in range(count)]


def shards(iterate, source, region, fixed_mask):
    far = pl.BlockSpec(memory_space=pltpu.HBM)
    cells = (ZC, YC, 128)
    arguments = [
        pltpu.with_memory_space_constraint(argument, pltpu.HBM)
        for argument in (iterate, source, region, fixed_mask)
    ]
    edge = (2, ZC, 8, 128)
    zmsg, up, down = call(
        edge_kernel,
        (struct(5, YC, 128), struct(160, 128), struct(176, 128)),
        scratch=[
            pltpu.VMEM(edge, F32), pltpu.VMEM(edge, F32),
            pltpu.VMEM((2, 1, 8, 128), jnp.int32), pltpu.VMEM((2, 1, 8, 128), jnp.int32),
            pltpu.SemaphoreType.DMA((10,)),
        ],
        in_specs=[far] * 4,
    )(*arguments)
    lo = lax.ppermute(up, "gy", cyclic(GY, 1))
    hi = lax.ppermute(down, "gy", cyclic(GY, -1))
    zgot = lax.ppermute(zmsg, "gz", cyclic(GZ, 1))
    kept = (
        struct(GZ, 72, 128), struct(18, WIDE, 128), struct(ZC - 2, YC, 128),
        struct(3 * FR + 2 * YC, 128), struct(24 * FR, 128), struct(19, WIDE, 128),
        struct(18, FR, 128), struct(ZC, FR, 128), struct(2, FR, 128),
    )
    *state, frames = call(
        inner_kernel,
        kept,
        scratch=[
            pltpu.VMEM((1, YC, 128), jnp.int32), pltpu.VMEM((1, YC, 128), jnp.int32),
            pltpu.SemaphoreType.DMA((4,)),
        ],
        in_specs=[far] * 4,
        cost_estimate=COST,
    )(*arguments)
    lo, frames = lax.optimization_barrier((lo, frames))
    corners = call(corner_kernel, struct(56, 128))(lo, hi)
    corners = lax.ppermute(corners, "gz", cyclic(GZ, 1))
    state = call(
        halo_kernel, kept, cost_estimate=COST,
        input_output_aliases={3 + k: k for k in range(len(kept))},
    )(zgot, lo, hi, *state, frames)
    chunks, nu, resid, message, *_, frames = call(
        corner_residual_kernel, kept,
        input_output_aliases={1 + k: k for k in range(len(kept))},
    )(corners, *state)
    message = lax.ppermute(message, "gz", cyclic(GZ, -1))
    windows = lax.all_to_all(chunks, "gz", 0, 0, tiled=True)
    sent = call(
        modes_kernel,
        struct(GZ, 40, 128),
        scratch=[
            pltpu.VMEM((NZ, LANES), F32), pltpu.VMEM((NZ + 16, 384), F32),
        ],
    )(windows, *[jnp.asarray(table) for table in tables()])
    returned = lax.all_to_all(sent, "gz", 0, 0, tiled=True)
    zdir, image, sums = call(
        image_kernel,
        (struct(*cells), struct(*cells), struct(GZ * GY, 1, 128)),
        scratch=[pltpu.VMEM((18 * FR, 128), F32)],
    )(returned, nu, resid, message, frames)
    sums = lax.all_to_all(sums, ("gz", "gy"), 0, 0, tiled=True)
    correction, lin_residual, rms = call(
        output_kernel, (struct(*cells), struct(*cells), struct(1, 128))
    )(sums, zdir, image, resid, message)
    return correction, lin_residual, rms[0, 0]


def solution(mesh):
    placed = (P("gz", "gy", None),) * 4
    return jax.shard_map(
        shards,
        mesh=mesh,
        in_specs=placed,
        out_specs=(P("gz", "gy", None), P("gz", "gy", None), P()),
        check_vma=False,
    )
```

```python
import functools

import jax
import jax.numpy as jnp
import ml_dtypes
import numpy as np
from jax import lax
from jax.experimental import pallas as pl
from jax.experimental.pallas import tpu as pltpu
from jax.sharding import PartitionSpec as P

F32 = jnp.float32
BF16 = jnp.bfloat16
NZ, NY, NX = 512, 256, 128
GZ, GY = 32, 4
ZC, YC = NZ // GZ, NY // GY
FR = YC + 16
WIDE = FR + 16
WR, WC, RING = 23, 22, 3
LANES = 512
YP, XP = 4, 8
ROW0 = (0, 17, 33, 49)
VMEM_LIMIT = 40 * 1024 * 1024
COST = pl.CostEstimate(flops=4_000_000, bytes_accessed=8_000_000, transcendentals=0)


def segments(block):
    found = [(WC * (row // 4), row) for row in range(block, WR, 4)]
    if block < 3:
        found = [(0, found[-1][1]), (RING - block, found[0][1])] + found[1:]
    return found


def window_places():
    place = np.full((8, LANES), -1000, np.int32)
    for block in range(4):
        parts = segments(block) + [(128, None)]
        for (begin, row), (end, _) in zip(parts[:-1], parts[1:]):
            for lane in range(begin, end):
                column = (lane - WC * (row // 4)) % 128
                if column < WC:
                    place[0, 128 * block + lane] = row
                    place[1, 128 * block + lane] = column
    return place


def tables():
    index = np.arange(NZ, dtype=np.int64)
    phase = (index[:, None] + 1) * (index[None, :] + 1) % (2 * (NZ + 1))
    table = np.sqrt(2.0 / (NZ + 1)) * np.sin(np.pi * phase / (NZ + 1))
    table = table.astype(np.float32)
    high = table.astype(ml_dtypes.bfloat16)
    low = (table - high.astype(np.float32)).astype(ml_dtypes.bfloat16)
    lam = 2.0 - 2.0 * np.cos(np.pi * (index + 1.0) / (NZ + 1))
    lam = np.broadcast_to(lam.astype(np.float32)[:, None], (NZ, 128))
    there, back = [np.roll(t, 2, 1) for t in (high, low)], [np.roll(t, 2, 0) for t in (high, low)]
    return *there, *back, np.ascontiguousarray(lam), window_places()


def lane_iota(shape):
    return lax.broadcasted_iota(jnp.int32, shape, len(shape) - 1)


def roll(value, shift, axis):
    return pltpu.roll(value, shift % value.shape[axis], axis)


def start_all(pairs, sems):
    copies = [pltpu.make_async_copy(x, y, sems.at[k]) for k, (x, y) in enumerate(pairs)]
    for copy in copies:
        copy.start()
    return copies


def edge_kernel(it, src, reg, msk, zmsg, up, down, e_it, e_src, e_reg, e_msk, sems):
    pairs = [(it.at[ZC - 3:ZC], zmsg.at[0:3]), (src.at[ZC - 2:ZC], zmsg.at[3:5])]
    for side, row in enumerate((0, YC - 8)):
        rows = pl.ds(row, 8)
        pairs += [
            (it.at[:, rows], e_it.at[side]),
            (src.at[:, rows], e_src.at[side]),
            (reg.at[0:1, rows], e_reg.at[side]),
            (msk.at[0:1, rows], e_msk.at[side]),
        ]
    copies = start_all(pairs, sems)
    for copy in copies[2:]:
        copy.wait()
    for z in range(ZC):
        up[5 * z:5 * z + 5] = e_it[1, z, 3:8]
        down[6 * z:6 * z + 6] = e_it[0, z, 0:6]
        up[80 + 4 * z:84 + 4 * z] = e_src[1, z, 4:8]
        down[96 + 4 * z:100 + 4 * z] = e_src[0, z, 0:4]
    up[144:149] = e_reg[1, 0, 3:8].astype(F32)
    up[149:153] = e_msk[1, 0, 4:8].astype(F32)
    up[153:160] = jnp.zeros((7, 128), F32)
    down[160:165] = e_reg[0, 0, 0:5].astype(F32)
    down[165:169] = e_msk[0, 0, 0:4].astype(F32)
    down[169:176] = jnp.zeros((7, 128), F32)
    for copy in copies[:2]:
        copy.wait()


def corner_kernel(lo, hi, out):
    out[0:15] = lo[65:80]
    out[15:33] = hi[78:96]
    out[33:41] = lo[136:144]
    out[41:49] = hi[152:160]
    out[49:56] = jnp.zeros((7, 128), F32)


INNER, OUTER = ((8, YC),), ((0, 16), (YC, 16))


def edge_lanes(count):
    lane = lane_iota((count, 128))
    return lane == 0, lane == 127


def level(frame, p, span, shift=0):
    return frame[p, pl.ds(8 + span[0] + shift, span[1])]


def set_nu(p, span, field, right, nu, iron, last):
    u, uz = level(field, p, span), level(field, p + 1, span)
    if p == 2:
        uz = jnp.where(lax.axis_index("gz") == 0, 0.0, uz)
    ux = jnp.where(last, 0.0, roll(u, -1, 1))
    right[p, pl.ds(*span)] = ux
    dz = uz - u
    dy = level(field, p, span, 1) - u
    dx = ux - u
    bsq = dz * dz + dy * dy + dx * dx
    bsq = bsq * bsq
    nu[p, pl.ds(8 + span[0], span[1])] = jnp.where(iron, 0.05 + bsq / (bsq + 9.0), 1.0)


def set_residuals(span, steps, field, right, nu, drive, flat, rows, resid, first, last):
    start = lax.axis_index("gz") == 0
    begin, count = span
    copper, held = flat[0, pl.ds(*span)] == 1.0, flat[1, pl.ds(*span)] == 1.0
    own = max(begin, 8)
    own = slice(own - begin, min(begin + count, 8 + YC) - begin)
    kept = pl.ds(begin + own.start - 8, own.stop - own.start)
    p = steps[0]
    flux = 0.5 * (level(nu, p, span) + level(nu, p + 1, span)) * (
        level(field, p, span) - level(field, p + 1, span)
    )
    for t in steps:
        p = t + 1
        u, n = level(field, p, span), level(nu, p, span)
        uz, nz = level(field, p + 1, span), level(nu, p + 1, span)
        if p == 2:
            uz, nz = jnp.where(start, 0.0, uz), jnp.where(start, 1.0, nz)
        if p == 3:
            flux = jnp.where(start, -0.5 * (1.0 + n) * u, flux)
        ahead = 0.5 * (n + nz) * (u - uz)
        flow = ahead - flux
        flux = ahead
        flow = flow + 0.5 * (n + level(nu, p, span, 1)) * (u - level(field, p, span, 1))
        flow = flow + 0.5 * (n + level(nu, p, span, -1)) * (u - level(field, p, span, -1))
        nx = jnp.where(last, 1.0, roll(n, -1, 1))
        fx = 0.5 * (n + nx) * (u - right[p, pl.ds(*span)])
        flow = flow + (fx - jnp.where(first, -0.5 * (n + 1.0) * u, roll(fx, 1, 1)))
        value = -jnp.where(held, u, flow - jnp.where(copper, drive[t, pl.ds(*span)], 0.0))
        rows[pl.ds(t * FR + begin, count), :] = value
        resid[t, kept] = value[own]


def set_means(span, rows, first, last):
    begin, count = 16 * FR + span[0], span[1]
    total = rows[pl.ds(begin, count), :]
    rows[pl.ds(begin + FR, count), :] = 2.0 * total + 0.5 * (
        rows[pl.ds(begin - 1, count), :] + rows[pl.ds(begin + 1, count), :]
        + jnp.where(last, float(ZC), roll(total, -1, 1))
        + jnp.where(first, float(ZC), roll(total, 1, 1))
    )


def work(spans, planes, steps, field, right, nu, drive, flat, rows, resid):
    for span in spans:
        first, last = edge_lanes(span[1])
        iron = flat[0, pl.ds(*span)] == 2.0
        for p in planes:
            set_nu(p, span, field, right, nu, iron, last)
    for span in spans:
        first, last = edge_lanes(span[1])
        set_residuals(
            span, steps, field, right, nu, drive, flat, rows, resid, first, last
        )


def sum_planes(spans, nu, rows):
    for span in spans:
        total = level(nu, 1, span)
        for p in range(2, 17):
            total = total + level(nu, p, span)
        rows[pl.ds(16 * FR + span[0], span[1]), :] = total
    for span in spans:
        set_means(span, rows, *edge_lanes(span[1]))


def pack(rows, chunks, parts_y, tiles):
    lane = lane_iota((8, 128))
    places = [(lane - 16 * xp) & 127 for xp in range(XP)]
    for yp in parts_y:
        for block in range(4):
            parts = segments(block)
            turned = {}
            for begin, row in parts:
                at = ROW0[yp] + row + 4
                turned[row] = [
                    roll(
                        rows[pl.ds(8 * tile * FR + at, 8, stride=FR), :],
                        WC * (row // 4) + RING, 1,
                    )
                    for tile in tiles
                ]
            for xp in range(XP):
                values = turned[parts[0][1]]
                for begin, row in parts[1:]:
                    later = places[xp] >= begin
                    values = [jnp.where(later, x, y) for x, y in zip(turned[row], values)]
                peer, at = yp * XP + xp, 16 * block
                for tile, value in zip(tiles, values):
                    if tile < 2:
                        chunks[peer, at + 8 * tile:at + 8 * tile + 8, :] = value
                    else:
                        chunks[peer, 64 + 2 * block:66 + 2 * block, :] = value[0:2]


BEHIND, HERE = range(0, 3), range(3, 18)


def inner_kernel(it, src, reg, msk, chunks, nu, resid, rows, field, right, drive, flat,
                 reg_in, msk_in, sems):
    own = slice(8, 8 + YC)
    copies = start_all(
        (
            (it, field.at[3:19, 16:16 + YC]), (src.at[0:ZC - 2], drive.at[2:ZC, own]),
            (reg.at[0:1], reg_in), (msk.at[0:1], msk_in),
        ),
        sems,
    )
    rows[18 * FR:24 * FR, :] = jnp.zeros((6 * FR, 128), F32)
    for copy in copies:
        copy.wait()
    flat[0, own] = reg_in[0].astype(F32)
    flat[1, own] = msk_in[0].astype(F32)
    work(INNER, HERE, range(3, ZC), field, right, nu, drive, flat, rows, resid)
    pack(rows, chunks, (1, 2), (1,))


def halo_kernel(zgot, lo, hi, *refs):
    chunks, nu, resid, rows, field, right, drive, flat = refs[8:]
    column = lax.axis_index("gy")

    def below(value):
        return jnp.where(column == 0, 0.0, value)

    def above(value):
        return jnp.where(column == GY - 1, 0.0, value)

    for p in range(3):
        field[p, 16:16 + YC] = zgot[p]
    for z in range(ZC):
        field[z + 3, 11:16] = below(lo[5 * z:5 * z + 5])
        field[z + 3, 80:86] = above(hi[6 * z:6 * z + 6])
    for t in range(2):
        drive[t, 8:8 + YC] = zgot[3 + t]
    for z in range(ZC - 2):
        drive[z + 2, 4:8] = lo[80 + 4 * z:84 + 4 * z]
        drive[z + 2, 72:76] = hi[96 + 4 * z:100 + 4 * z]
    flat[0, 3:8] = below(lo[144:149])
    flat[0, 72:77] = above(hi[160:165])
    flat[1, 4:8] = lo[149:153]
    flat[1, 72:76] = hi[165:169]
    work(INNER, BEHIND, range(0, 3), field, right, nu, drive, flat, rows, resid)
    work(OUTER, HERE, range(3, ZC), field, right, nu, drive, flat, rows, resid)
    sum_planes(INNER, nu, rows)
    pack(rows, chunks, (1, 2), (0, 2))
    pack(rows, chunks, (0, 3), (1,))


def corner_residual_kernel(corners, *refs):
    chunks, nu, resid, rows, field, right, drive, flat = refs[8:]
    column = lax.axis_index("gy")
    for p in range(3):
        field[p, 11:16] = jnp.where(column == 0, 0.0, corners[5 * p:5 * p + 5])
        field[p, 80:86] = jnp.where(column == GY - 1, 0.0, corners[15 + 6 * p:21 + 6 * p])
    for t in range(2):
        drive[t, 4:8] = corners[33 + 4 * t:37 + 4 * t]
        drive[t, 72:76] = corners[41 + 4 * t:45 + 4 * t]
    work(OUTER, BEHIND, range(0, 3), field, right, nu, drive, flat, rows, resid)
    sum_planes(OUTER, nu, rows)
    pack(rows, chunks, (0, 3), (0, 2))


def product(high, low, right_high, right_low):
    left = jnp.concatenate([high, low, high], axis=1)
    right = jnp.concatenate([right_high, right_high, right_low], axis=0)
    return jnp.dot(left, right, preferred_element_type=F32)


def modes_kernel(got, ahead_high, ahead_low, high, low, lam, spots, out, lines, back):
    group, column = lax.axis_index("gz"), lax.axis_index("gy")
    yp, xp = lax.div(group, XP), lax.rem(group, XP)
    s_high, s_low = ahead_high[...], ahead_low[...]
    for half in range(2):
        value = jnp.concatenate(
            [
                got[:, 16 * block:16 * block + 16, :].reshape(NZ, 128)
                for block in (2 * half, 2 * half + 1)
            ],
            axis=1,
        )
        v_high = value.astype(BF16)
        v_low = (value - v_high.astype(F32)).astype(BF16)
        lines[:, 256 * half:256 * half + 256] = product(s_high, s_low, v_high, v_low)

    sums = jnp.sum(got[:, 64:72, :], axis=0) * (1.0 / NZ)
    mean = [sums[2 * b:2 * b + 1] for b in range(4)]
    faces = [sums[2 * b + 1:2 * b + 2] for b in range(4)]
    turned = [pltpu.roll(spots[:, 128 * b:128 * b + 128], 16 * xp, 1) for b in range(4)]
    row = jnp.concatenate([place[0:1] for place in turned], axis=1)
    col = jnp.concatenate([place[1:2] for place in turned], axis=1)
    ypos = column * YC + 16 * yp + jnp.where(yp > 0, 1, 0) + row - 4
    xpos = 16 * xp - RING + col
    inside = (row >= 0) & (xpos >= 0) & (xpos < NX) & (ypos >= 0) & (ypos < NY)
    right = [0.5 * (m + roll(m, -1, 1)) for m in mean]
    left = [roll(r, 1, 1) for r in right]
    above = [0.5 * (mean[b] + mean[b + 1]) for b in range(3)]
    above.append(0.5 * (mean[3] + roll(mean[0], -WC, 1)))
    below = [roll(above[3], WC, 1)] + above[:3]

    spot = lane_iota((LANES, 384))
    own = jnp.where(yp == 0, 1, 0)
    halo = jnp.where(yp == 0, 0, 16)
    inner = (spot - 16 * xp) & 127
    line = RING + jnp.where(spot < 256, own + 8 * (spot >> 7) + (inner >> 4), halo)
    pick = 128 * (line & 3) + ((WC * (line >> 2) + RING + (spot & 15) + 16 * xp) & 127)
    choose = jnp.where(lax.broadcasted_iota(jnp.int32, (LANES, 384), 0) == pick, 1.0, 0.0)
    choose = choose.astype(BF16)
    s_high, s_low = high[...], low[...]
    total = None
    for start in range(0, NZ, 128):
        part = slice(start, start + 128)
        lam_rows = lam[part, :]
        vhat = [lines[part, 128 * b:128 * b + 128] for b in range(4)]
        factor = [
            jnp.where(inside[:, 128 * b:128 * b + 128], 0.6 / (faces[b] + lam_rows * mean[b]), 0.0)
            for b in range(4)
        ]
        w = [factor[b] * vhat[b] for b in range(4)]
        for _ in range(3):
            after = w[1:] + [roll(w[0], -WC, 1)]
            before = [roll(w[3], WC, 1)] + w[:3]
            near = [
                above[b] * after[b] + below[b] * before[b]
                + right[b] * roll(w[b], -1, 1) + left[b] * roll(w[b], 1, 1)
                for b in range(4)
            ]
            w = [0.4 * w[b] + factor[b] * (vhat[b] + near[b]) for b in range(4)]
        w = jnp.concatenate(w, axis=1)
        w_high = w.astype(BF16)
        w_low = (w - w_high.astype(F32)).astype(BF16)
        w_high = jnp.dot(w_high, choose, preferred_element_type=F32).astype(BF16)
        w_low = jnp.dot(w_low, choose, preferred_element_type=F32).astype(BF16)
        term = product(high[:, part], low[:, part], w_high, w_low)
        total = term if total is None else total + term
    back[8:8 + NZ, :] = total
    back[0:8, :] = total[NZ - 8:]
    back[8 + NZ:, :] = total[:8]

    sub = lax.broadcasted_iota(jnp.int32, (8, 128), 0)
    pattern = (((lane_iota((8, 128)) >> 4) + sub - xp) & 7) == 0
    for peer in range(GZ):
        at = 8 + ZC * peer
        for block in range(2):
            lanes = slice(128 * block, 128 * block + 128)
            out[peer, 16 * block:16 * block + 16, :] = back[at:at + ZC, lanes]
            out[peer, 32 + block:33 + block, :] = back[at - 1:at, lanes]
            out[peer, 34 + block:35 + block, :] = back[at + ZC:at + ZC + 1, lanes]
            piece = back[at + 8 * block:at + 8 * block + 8, 256:384]
            piece = jnp.sum(jnp.where(pattern, piece, 0.0), axis=0, keepdims=True)
            out[peer, 36 + block:37 + block, :] = piece
            out[peer, 38 + block:39 + block, :] = back[at + ZC + 1:at + ZC + 2, lanes]


def image_kernel(got, nu, resid, flat, zdir, image, message, sums, frame):
    lane = lane_iota((8, 128))
    places = [(lane >> 4) == k for k in range(8)]

    def spread(tiles, jj):
        value = tiles[0]
        for xp in range(1, XP):
            value = jnp.where(places[(jj + xp) % 8], tiles[xp], value)
        return roll(value, -16 * jj, 1)

    for yp in range(YP):
        for block in range(2):
            for tile in range(2):
                at = 16 * block + 8 * tile
                tiles = [got[yp * XP + xp, at:at + 8, :] for xp in range(XP)]
                for jj in range(8):
                    y = 8 + 16 * yp + 8 * block + jj
                    frame[pl.ds((1 + 8 * tile) * FR + y, 8, stride=FR), :] = spread(tiles, jj)
        tiles = [got[yp * XP + xp, 32:40, :] for xp in range(XP)]
        for jj in range(8):
            value = spread(tiles, jj)
            y = 8 + 16 * yp + jj
            for k in range(2):
                frame[y + 8 * k:y + 8 * k + 1, :] = value[k:k + 1]
                for p, row in ((17, 2), (18, 6)):
                    at = p * FR + y + 8 * k
                    frame[at:at + 1, :] = value[row + k:row + k + 1]

    sub = lax.broadcasted_iota(jnp.int32, (8, 128), 0)
    turn = ((lane >> 4) + sub) & 7
    for yp, y in ((0, 7), (YP - 1, 8 + YC)):
        for tile in range(2):
            value = jnp.zeros((8, 128), F32)
            for xp in range(XP):
                line = got[yp * XP + xp, 36 + tile:37 + tile, :]
                value = jnp.where(turn == xp, jnp.broadcast_to(line, (8, 128)), value)
            value = pltpu.roll(value, 0, 1, stride=16, stride_axis=0)
            frame[pl.ds((1 + 8 * tile) * FR + y, 8, stride=FR), :] = value

    lane = lane_iota((YC, 128))
    first, last = lane == 0, lane == 127
    held = flat[1, 8:8 + YC] == 1.0

    start = lax.axis_index("gz") == 0

    def nu_rows(p, shift=0):
        return nu[p, 16 + shift:16 + shift + YC]

    def dir_rows(p, shift=0):
        at = p * FR + 8 + shift
        return frame[at:at + YC, :]

    d, n = dir_rows(1), nu_rows(1)
    flux = 0.5 * (nu_rows(0) + n) * (dir_rows(0) - d)
    rr = ri = ii = jnp.zeros((8, 128), F32)

    def fold(value):
        return jnp.sum(value.reshape(YC // 8, 8, 128), axis=0)

    for t in range(ZC):
        p = t + 1
        dz, nz = dir_rows(p + 1), nu_rows(p + 1)
        up, nup = dz, nz
        if p == 2:
            up, nup = jnp.where(start, 0.0, dz), jnp.where(start, 1.0, nz)
        if p == 3:
            flux = jnp.where(start, -0.5 * (1.0 + n) * d, flux)
        ahead = 0.5 * (n + nup) * (d - up)
        flow = ahead - flux
        flow = flow + 0.5 * (n + nu_rows(p, 1)) * (d - dir_rows(p, 1))
        flow = flow + 0.5 * (n + nu_rows(p, -1)) * (d - dir_rows(p, -1))
        nx = jnp.where(last, 1.0, roll(n, -1, 1))
        dx = jnp.where(last, 0.0, roll(d, -1, 1))
        fx = 0.5 * (n + nx) * (d - dx)
        flow = flow + (fx - jnp.where(first, -0.5 * (n + 1.0) * d, roll(fx, 1, 1)))
        value = jnp.where(held, d, flow)
        r = resid[t]
        zdir[t] = d
        image[t] = value
        if t < 2:
            message[t], message[2 + t] = value, r
        rr, ri, ii = rr + fold(r * r), ri + fold(r * value), ii + fold(value * value)
        d, n, flux = dz, nz, ahead

    zdir[ZC], zdir[ZC + 1] = dir_rows(ZC + 1), dir_rows(ZC + 2)
    parts = (rr, ri, ii)
    line = lane_iota((1, 128))
    packed = jnp.zeros((1, 128), F32)
    for k, part in enumerate(parts):
        packed = jnp.where(line == k, jnp.sum(part), packed)
    sums[...] = jnp.broadcast_to(packed[None], sums.shape)


def output_kernel(sums, zdir, image, resid, message, correction, lin_residual, rms):
    total = jnp.sum(sums[...], axis=0)
    beta_sq = total[0:1, 0:1] + 1e-06
    beta = jnp.sqrt(beta_sq)
    h_one = total[0:1, 1:2] / beta_sq
    denom = total[0:1, 2:3] / beta_sq - h_one * h_one * (1e-06 / beta_sq) + 1e-06
    gamma = h_one / denom
    correction[...] = zdir[2:] * gamma[None]
    lin_residual[0:ZC - 2] = resid[2:] - gamma[None] * image[2:]
    lin_residual[ZC - 2:ZC] = message[2:4] - gamma[None] * message[0:2]
    rms[...] = jnp.broadcast_to(beta * (1.0 / np.sqrt(float(NZ * NY * NX))), rms.shape)


def call(kernel, out_shape, scratch=(), **extra):
    return pl.pallas_call(
        kernel,
        out_shape=out_shape,
        scratch_shapes=scratch,
        compiler_params=pltpu.CompilerParams(vmem_limit_bytes=VMEM_LIMIT),
        **extra,
    )


def struct(*shape):
    return jax.ShapeDtypeStruct(shape, F32)


def cyclic(count, step):
    return [(i, (i + step) % count) for i in range(count)]


def shards(iterate, source, region, fixed_mask):
    far = pl.BlockSpec(memory_space=pltpu.HBM)
    cells = (ZC, YC, 128)
    arguments = [
        pltpu.with_memory_space_constraint(argument, pltpu.HBM)
        for argument in (iterate, source, region, fixed_mask)
    ]
    edge = (2, ZC, 8, 128)
    zmsg, up, down = call(
        edge_kernel,
        (struct(5, YC, 128), struct(160, 128), struct(176, 128)),
        scratch=[
            pltpu.VMEM(edge, F32), pltpu.VMEM(edge, F32),
            pltpu.VMEM((2, 1, 8, 128), jnp.int32), pltpu.VMEM((2, 1, 8, 128), jnp.int32),
            pltpu.SemaphoreType.DMA((10,)),
        ],
        in_specs=[far] * 4,
    )(*arguments)
    lo = lax.ppermute(up, "gy", cyclic(GY, 1))
    hi = lax.ppermute(down, "gy", cyclic(GY, -1))
    zgot = lax.ppermute(zmsg, "gz", cyclic(GZ, 1))
    kept = (
        struct(GZ, 72, 128), struct(18, WIDE, 128), struct(*cells), struct(24 * FR, 128),
        struct(19, WIDE, 128), struct(18, FR, 128), struct(ZC, FR, 128), struct(2, FR, 128),
    )
    *state, frames = call(
        inner_kernel,
        kept,
        scratch=[
            pltpu.VMEM((1, YC, 128), jnp.int32), pltpu.VMEM((1, YC, 128), jnp.int32),
            pltpu.SemaphoreType.DMA((4,)),
        ],
        in_specs=[far] * 4,
        cost_estimate=COST,
    )(*arguments)
    lo, frames = lax.optimization_barrier((lo, frames))
    corners = call(corner_kernel, struct(56, 128))(lo, hi)
    corners = lax.ppermute(corners, "gz", cyclic(GZ, 1))
    state = call(
        halo_kernel, kept, cost_estimate=COST,
        input_output_aliases={3 + k: k for k in range(len(kept))},
    )(zgot, lo, hi, *state, frames)
    chunks, nu, resid, *_, frames = call(
        corner_residual_kernel, kept,
        input_output_aliases={1 + k: k for k in range(len(kept))},
    )(corners, *state)
    windows = lax.all_to_all(chunks, "gz", 0, 0, tiled=True)
    sent = call(
        modes_kernel,
        struct(GZ, 40, 128),
        scratch=[
            pltpu.VMEM((NZ, LANES), F32), pltpu.VMEM((NZ + 16, 384), F32),
        ],
    )(windows, *[jnp.asarray(table) for table in tables()])
    returned = lax.all_to_all(sent, "gz", 0, 0, tiled=True)
    zdir, image, message, sums = call(
        image_kernel,
        (
            struct(ZC + 2, YC, 128), struct(*cells), struct(4, YC, 128),
            struct(GZ * GY, 1, 128),
        ),
        scratch=[pltpu.VMEM((19 * FR, 128), F32)],
    )(returned, nu, resid, frames)
    message = lax.ppermute(message, "gz", cyclic(GZ, -1))
    sums = lax.all_to_all(sums, ("gz", "gy"), 0, 0, tiled=True)
    correction, lin_residual, rms = call(
        output_kernel, (struct(*cells), struct(*cells), struct(1, 128))
    )(sums, zdir, image, resid, message)
    return correction, lin_residual, rms[0, 0]


def solution(mesh):
    placed = (P("gz", "gy", None),) * 4
    return jax.shard_map(
        shards,
        mesh=mesh,
        in_specs=placed,
        out_specs=(P("gz", "gy", None), P("gz", "gy", None), P()),
        check_vma=False,
    )
```

```python
import functools

import jax
import jax.numpy as jnp
import ml_dtypes
import numpy as np
from jax import lax
from jax.experimental import pallas as pl
from jax.experimental.pallas import tpu as pltpu
from jax.sharding import PartitionSpec as P

F32 = jnp.float32
BF16 = jnp.bfloat16
NZ, NY, NX = 512, 256, 128
GZ, GY = 32, 4
ZC, YC = NZ // GZ, NY // GY
FR = YC + 16
WIDE = FR + 16
WR, WC, RING = 23, 22, 3
LANES = 512
YP, XP = 4, 8
ROW0 = (0, 17, 33, 49)
VMEM_LIMIT = 40 * 1024 * 1024
COST = pl.CostEstimate(flops=4_000_000, bytes_accessed=8_000_000, transcendentals=0)


def segments(block):
    found = [(WC * (row // 4), row) for row in range(block, WR, 4)]
    if block < 3:
        found = [(0, found[-1][1]), (RING - block, found[0][1])] + found[1:]
    return found


def window_places():
    place = np.full((8, LANES), -1000, np.int32)
    for block in range(4):
        parts = segments(block) + [(128, None)]
        for (begin, row), (end, _) in zip(parts[:-1], parts[1:]):
            for lane in range(begin, end):
                column = (lane - WC * (row // 4)) % 128
                if column < WC:
                    place[0, 128 * block + lane] = row
                    place[1, 128 * block + lane] = column
    return place


def tables():
    index = np.arange(NZ, dtype=np.int64)
    phase = (index[:, None] + 1) * (index[None, :] + 1) % (2 * (NZ + 1))
    table = np.sqrt(2.0 / (NZ + 1)) * np.sin(np.pi * phase / (NZ + 1))
    table = table.astype(np.float32)
    high = table.astype(ml_dtypes.bfloat16)
    low = (table - high.astype(np.float32)).astype(ml_dtypes.bfloat16)
    lam = 2.0 - 2.0 * np.cos(np.pi * (index + 1.0) / (NZ + 1))
    lam = np.broadcast_to(lam.astype(np.float32)[:, None], (NZ, 128))
    there, back = [np.roll(t, 2, 1) for t in (high, low)], [np.roll(t, 2, 0) for t in (high, low)]
    return *there, *back, np.ascontiguousarray(lam), window_places()


def lane_iota(shape):
    return lax.broadcasted_iota(jnp.int32, shape, len(shape) - 1)


def roll(value, shift, axis):
    return pltpu.roll(value, shift % value.shape[axis], axis)


def start_all(pairs, sems):
    copies = [pltpu.make_async_copy(x, y, sems.at[k]) for k, (x, y) in enumerate(pairs)]
    for copy in copies:
        copy.start()
    return copies


def edge_kernel(it, src, reg, msk, z_one, z_two, up, down, e_it, e_src, e_reg, e_msk, sems):
    half = YC // 2
    pairs = [
        (it.at[ZC - 3], z_one.at[0:YC]), (it.at[ZC - 2], z_one.at[YC:2 * YC]),
        (it.at[ZC - 1, 0:half], z_one.at[2 * YC:]), (it.at[ZC - 1, half:], z_two.at[0:half]),
        (src.at[ZC - 2], z_two.at[half:half + YC]), (src.at[ZC - 1], z_two.at[half + YC:]),
    ]
    for side, row in enumerate((0, YC - 8)):
        rows = pl.ds(row, 8)
        pairs += [
            (it.at[:, rows], e_it.at[side]),
            (src.at[:, rows], e_src.at[side]),
            (reg.at[0:1, rows], e_reg.at[side]),
            (msk.at[0:1, rows], e_msk.at[side]),
        ]
    copies = start_all(pairs, sems)
    for copy in copies[6:]:
        copy.wait()
    for z in range(ZC):
        up[5 * z:5 * z + 5] = e_it[1, z, 3:8]
        down[6 * z:6 * z + 6] = e_it[0, z, 0:6]
        up[80 + 4 * z:84 + 4 * z] = e_src[1, z, 4:8]
        down[96 + 4 * z:100 + 4 * z] = e_src[0, z, 0:4]
    up[144:149] = e_reg[1, 0, 3:8].astype(F32)
    up[149:153] = e_msk[1, 0, 4:8].astype(F32)
    up[153:176] = jnp.zeros((23, 128), F32)
    down[160:165] = e_reg[0, 0, 0:5].astype(F32)
    down[165:169] = e_msk[0, 0, 0:4].astype(F32)
    down[169:176] = jnp.zeros((7, 128), F32)
    for copy in copies[:6]:
        copy.wait()


def corner_kernel(lo, hi, out):
    out[0:15] = lo[65:80]
    out[15:33] = hi[78:96]
    out[33:41] = lo[136:144]
    out[41:49] = hi[152:160]
    out[49:56] = jnp.zeros((7, 128), F32)


INNER, OUTER = ((8, YC),), ((0, 16), (YC, 16))


def edge_lanes(count):
    lane = lane_iota((count, 128))
    return lane == 0, lane == 127


def level(frame, p, span, shift=0):
    return frame[p, pl.ds(8 + span[0] + shift, span[1])]


def set_nu(p, span, field, right, nu, iron, last):
    u, uz = level(field, p, span), level(field, p + 1, span)
    if p == 2:
        uz = jnp.where(lax.axis_index("gz") == 0, 0.0, uz)
    ux = jnp.where(last, 0.0, roll(u, -1, 1))
    right[p, pl.ds(*span)] = ux
    dz = uz - u
    dy = level(field, p, span, 1) - u
    dx = ux - u
    bsq = dz * dz + dy * dy + dx * dx
    bsq = bsq * bsq
    nu[p, pl.ds(8 + span[0], span[1])] = jnp.where(iron, 0.05 + bsq / (bsq + 9.0), 1.0)


def set_residuals(span, steps, field, right, nu, drive, flat, rows, resid, first, last):
    start = lax.axis_index("gz") == 0
    begin, count = span
    copper, held = flat[0, pl.ds(*span)] == 1.0, flat[1, pl.ds(*span)] == 1.0
    own = max(begin, 8)
    own = slice(own - begin, min(begin + count, 8 + YC) - begin)
    kept = pl.ds(begin + own.start - 8, own.stop - own.start)
    p = steps[0]
    flux = 0.5 * (level(nu, p, span) + level(nu, p + 1, span)) * (
        level(field, p, span) - level(field, p + 1, span)
    )
    for t in steps:
        p = t + 1
        u, n = level(field, p, span), level(nu, p, span)
        uz, nz = level(field, p + 1, span), level(nu, p + 1, span)
        if p == 2:
            uz, nz = jnp.where(start, 0.0, uz), jnp.where(start, 1.0, nz)
        if p == 3:
            flux = jnp.where(start, -0.5 * (1.0 + n) * u, flux)
        ahead = 0.5 * (n + nz) * (u - uz)
        flow = ahead - flux
        flux = ahead
        flow = flow + 0.5 * (n + level(nu, p, span, 1)) * (u - level(field, p, span, 1))
        flow = flow + 0.5 * (n + level(nu, p, span, -1)) * (u - level(field, p, span, -1))
        nx = jnp.where(last, 1.0, roll(n, -1, 1))
        fx = 0.5 * (n + nx) * (u - right[p, pl.ds(*span)])
        flow = flow + (fx - jnp.where(first, -0.5 * (n + 1.0) * u, roll(fx, 1, 1)))
        value = -jnp.where(held, u, flow - jnp.where(copper, drive[t, pl.ds(*span)], 0.0))
        rows[pl.ds(t * FR + begin, count), :] = value
        resid[t, kept] = value[own]


def set_means(span, rows, first, last):
    begin, count = 16 * FR + span[0], span[1]
    total = rows[pl.ds(begin, count), :]
    rows[pl.ds(begin + FR, count), :] = 2.0 * total + 0.5 * (
        rows[pl.ds(begin - 1, count), :] + rows[pl.ds(begin + 1, count), :]
        + jnp.where(last, float(ZC), roll(total, -1, 1))
        + jnp.where(first, float(ZC), roll(total, 1, 1))
    )


def work(spans, planes, steps, field, right, nu, drive, flat, rows, resid):
    for span in spans:
        first, last = edge_lanes(span[1])
        iron = flat[0, pl.ds(*span)] == 2.0
        for p in planes:
            set_nu(p, span, field, right, nu, iron, last)
    for span in spans:
        first, last = edge_lanes(span[1])
        set_residuals(
            span, steps, field, right, nu, drive, flat, rows, resid, first, last
        )


def sum_planes(spans, nu, rows):
    for span in spans:
        total = level(nu, 1, span)
        for p in range(2, 17):
            total = total + level(nu, p, span)
        rows[pl.ds(16 * FR + span[0], span[1]), :] = total
    for span in spans:
        set_means(span, rows, *edge_lanes(span[1]))


def pack(rows, chunks, parts_y, tiles):
    lane = lane_iota((8, 128))
    places = [(lane - 16 * xp) & 127 for xp in range(XP)]
    for yp in parts_y:
        for block in range(4):
            parts = segments(block)
            turned = {}
            for begin, row in parts:
                at = ROW0[yp] + row + 4
                turned[row] = [
                    roll(
                        rows[pl.ds(8 * tile * FR + at, 8, stride=FR), :],
                        WC * (row // 4) + RING, 1,
                    )
                    for tile in tiles
                ]
            for xp in range(XP):
                values = turned[parts[0][1]]
                for begin, row in parts[1:]:
                    later = places[xp] >= begin
                    values = [jnp.where(later, x, y) for x, y in zip(turned[row], values)]
                peer, at = yp * XP + xp, 16 * block
                for tile, value in zip(tiles, values):
                    if tile < 2:
                        chunks[peer, at + 8 * tile:at + 8 * tile + 8, :] = value
                    else:
                        chunks[peer, 64 + 2 * block:66 + 2 * block, :] = value[0:2]


BEHIND, HERE = range(0, 3), range(3, 18)


def inner_kernel(it, src, reg, msk, chunks, nu, resid, rows, field, right, drive, flat,
                 reg_in, msk_in, sems):
    own = slice(8, 8 + YC)
    copies = start_all(
        (
            (it, field.at[3:19, 16:16 + YC]), (src.at[0:ZC - 2], drive.at[2:ZC, own]),
            (reg.at[0:1], reg_in), (msk.at[0:1], msk_in),
        ),
        sems,
    )
    rows[18 * FR:24 * FR, :] = jnp.zeros((6 * FR, 128), F32)
    for copy in copies:
        copy.wait()
    flat[0, own] = reg_in[0].astype(F32)
    flat[1, own] = msk_in[0].astype(F32)
    work(INNER, HERE, range(3, ZC), field, right, nu, drive, flat, rows, resid)
    pack(rows, chunks, (1, 2), (1,))


def halo_kernel(z_one, z_two, lo, hi, *refs):
    chunks, nu, resid, rows, field, right, drive, flat = refs[8:]
    column = lax.axis_index("gy")

    def below(value):
        return jnp.where(column == 0, 0.0, value)

    def above(value):
        return jnp.where(column == GY - 1, 0.0, value)

    half = YC // 2
    field[0, 16:16 + YC] = z_one[0:YC]
    field[1, 16:16 + YC] = z_one[YC:2 * YC]
    field[2, 16:16 + half] = z_one[2 * YC:]
    field[2, 16 + half:16 + YC] = z_two[0:half]
    for z in range(ZC):
        field[z + 3, 11:16] = below(lo[5 * z:5 * z + 5])
        field[z + 3, 80:86] = above(hi[6 * z:6 * z + 6])
    for t in range(2):
        drive[t, 8:8 + YC] = z_two[half + YC * t:half + YC * t + YC]
    for z in range(ZC - 2):
        drive[z + 2, 4:8] = lo[80 + 4 * z:84 + 4 * z]
        drive[z + 2, 72:76] = hi[96 + 4 * z:100 + 4 * z]
    flat[0, 3:8] = below(lo[144:149])
    flat[0, 72:77] = above(hi[160:165])
    flat[1, 4:8] = lo[149:153]
    flat[1, 72:76] = hi[165:169]
    work(INNER, BEHIND, range(0, 3), field, right, nu, drive, flat, rows, resid)
    work(OUTER, HERE, range(3, ZC), field, right, nu, drive, flat, rows, resid)
    sum_planes(INNER, nu, rows)
    pack(rows, chunks, (1, 2), (0, 2))
    pack(rows, chunks, (0, 3), (1,))


def corner_residual_kernel(corners, *refs):
    chunks, nu, resid, rows, field, right, drive, flat = refs[8:]
    column = lax.axis_index("gy")
    for p in range(3):
        field[p, 11:16] = jnp.where(column == 0, 0.0, corners[5 * p:5 * p + 5])
        field[p, 80:86] = jnp.where(column == GY - 1, 0.0, corners[15 + 6 * p:21 + 6 * p])
    for t in range(2):
        drive[t, 4:8] = corners[33 + 4 * t:37 + 4 * t]
        drive[t, 72:76] = corners[41 + 4 * t:45 + 4 * t]
    work(OUTER, BEHIND, range(0, 3), field, right, nu, drive, flat, rows, resid)
    sum_planes(OUTER, nu, rows)
    pack(rows, chunks, (0, 3), (0, 2))


def product(high, low, right_high, right_low):
    left = jnp.concatenate([high, low, high], axis=1)
    right = jnp.concatenate([right_high, right_high, right_low], axis=0)
    return jnp.dot(left, right, preferred_element_type=F32)


def modes_kernel(got, ahead_high, ahead_low, high, low, lam, spots, out, lines, back):
    group, column = lax.axis_index("gz"), lax.axis_index("gy")
    yp, xp = lax.div(group, XP), lax.rem(group, XP)
    s_high, s_low = ahead_high[...], ahead_low[...]
    for half in range(2):
        value = jnp.concatenate(
            [
                got[:, 16 * block:16 * block + 16, :].reshape(NZ, 128)
                for block in (2 * half, 2 * half + 1)
            ],
            axis=1,
        )
        v_high = value.astype(BF16)
        v_low = (value - v_high.astype(F32)).astype(BF16)
        lines[:, 256 * half:256 * half + 256] = product(s_high, s_low, v_high, v_low)

    sums = jnp.sum(got[:, 64:72, :], axis=0) * (1.0 / NZ)
    mean = [sums[2 * b:2 * b + 1] for b in range(4)]
    faces = [sums[2 * b + 1:2 * b + 2] for b in range(4)]
    turned = [pltpu.roll(spots[:, 128 * b:128 * b + 128], 16 * xp, 1) for b in range(4)]
    row = jnp.concatenate([place[0:1] for place in turned], axis=1)
    col = jnp.concatenate([place[1:2] for place in turned], axis=1)
    ypos = column * YC + 16 * yp + jnp.where(yp > 0, 1, 0) + row - 4
    xpos = 16 * xp - RING + col
    inside = (row >= 0) & (xpos >= 0) & (xpos < NX) & (ypos >= 0) & (ypos < NY)
    right = [0.5 * (m + roll(m, -1, 1)) for m in mean]
    left = [roll(r, 1, 1) for r in right]
    above = [0.5 * (mean[b] + mean[b + 1]) for b in range(3)]
    above.append(0.5 * (mean[3] + roll(mean[0], -WC, 1)))
    below = [roll(above[3], WC, 1)] + above[:3]

    spot = lane_iota((LANES, 384))
    own = jnp.where(yp == 0, 1, 0)
    halo = jnp.where(yp == 0, 0, 16)
    inner = (spot - 16 * xp) & 127
    line = RING + jnp.where(spot < 256, own + 8 * (spot >> 7) + (inner >> 4), halo)
    pick = 128 * (line & 3) + ((WC * (line >> 2) + RING + (spot & 15) + 16 * xp) & 127)
    choose = jnp.where(lax.broadcasted_iota(jnp.int32, (LANES, 384), 0) == pick, 1.0, 0.0)
    choose = choose.astype(BF16)
    s_high, s_low = high[...], low[...]
    total = None
    for start in range(0, NZ, 128):
        part = slice(start, start + 128)
        lam_rows = lam[part, :]
        vhat = [lines[part, 128 * b:128 * b + 128] for b in range(4)]
        factor = [
            jnp.where(inside[:, 128 * b:128 * b + 128], 0.6 / (faces[b] + lam_rows * mean[b]), 0.0)
            for b in range(4)
        ]
        w = [factor[b] * vhat[b] for b in range(4)]
        for _ in range(3):
            after = w[1:] + [roll(w[0], -WC, 1)]
            before = [roll(w[3], WC, 1)] + w[:3]
            near = [
                above[b] * after[b] + below[b] * before[b]
                + right[b] * roll(w[b], -1, 1) + left[b] * roll(w[b], 1, 1)
                for b in range(4)
            ]
            w = [0.4 * w[b] + factor[b] * (vhat[b] + near[b]) for b in range(4)]
        w = jnp.concatenate(w, axis=1)
        w_high = w.astype(BF16)
        w_low = (w - w_high.astype(F32)).astype(BF16)
        w_high = jnp.dot(w_high, choose, preferred_element_type=F32).astype(BF16)
        w_low = jnp.dot(w_low, choose, preferred_element_type=F32).astype(BF16)
        term = product(high[:, part], low[:, part], w_high, w_low)
        total = term if total is None else total + term
    back[8:8 + NZ, :] = total
    back[0:8, :] = total[NZ - 8:]
    back[8 + NZ:, :] = total[:8]

    sub = lax.broadcasted_iota(jnp.int32, (8, 128), 0)
    pattern = (((lane_iota((8, 128)) >> 4) + sub - xp) & 7) == 0
    for peer in range(GZ):
        at = 8 + ZC * peer
        for block in range(2):
            lanes = slice(128 * block, 128 * block + 128)
            out[peer, 16 * block:16 * block + 16, :] = back[at:at + ZC, lanes]
            out[peer, 32 + block:33 + block, :] = back[at - 1:at, lanes]
            out[peer, 34 + block:35 + block, :] = back[at + ZC:at + ZC + 1, lanes]
            piece = back[at + 8 * block:at + 8 * block + 8, 256:384]
            piece = jnp.sum(jnp.where(pattern, piece, 0.0), axis=0, keepdims=True)
            out[peer, 36 + block:37 + block, :] = piece
            out[peer, 38 + block:39 + block, :] = back[at + ZC + 1:at + ZC + 2, lanes]


def image_kernel(got, nu, resid, flat, zdir, image, message, sums, frame):
    lane = lane_iota((8, 128))
    places = [(lane >> 4) == k for k in range(8)]

    def spread(tiles, jj):
        value = tiles[0]
        for xp in range(1, XP):
            value = jnp.where(places[(jj + xp) % 8], tiles[xp], value)
        return roll(value, -16 * jj, 1)

    for yp in range(YP):
        for block in range(2):
            for tile in range(2):
                at = 16 * block + 8 * tile
                tiles = [got[yp * XP + xp, at:at + 8, :] for xp in range(XP)]
                for jj in range(8):
                    y = 8 + 16 * yp + 8 * block + jj
                    frame[pl.ds((1 + 8 * tile) * FR + y, 8, stride=FR), :] = spread(tiles, jj)
        tiles = [got[yp * XP + xp, 32:40, :] for xp in range(XP)]
        for jj in range(8):
            value = spread(tiles, jj)
            y = 8 + 16 * yp + jj
            for k in range(2):
                frame[y + 8 * k:y + 8 * k + 1, :] = value[k:k + 1]
                for p, row in ((17, 2), (18, 6)):
                    at = p * FR + y + 8 * k
                    frame[at:at + 1, :] = value[row + k:row + k + 1]

    sub = lax.broadcasted_iota(jnp.int32, (8, 128), 0)
    turn = ((lane >> 4) + sub) & 7
    for yp, y in ((0, 7), (YP - 1, 8 + YC)):
        for tile in range(2):
            value = jnp.zeros((8, 128), F32)
            for xp in range(XP):
                line = got[yp * XP + xp, 36 + tile:37 + tile, :]
                value = jnp.where(turn == xp, jnp.broadcast_to(line, (8, 128)), value)
            value = pltpu.roll(value, 0, 1, stride=16, stride_axis=0)
            frame[pl.ds((1 + 8 * tile) * FR + y, 8, stride=FR), :] = value

    lane = lane_iota((YC, 128))
    first, last = lane == 0, lane == 127
    held = flat[1, 8:8 + YC] == 1.0

    start = lax.axis_index("gz") == 0

    def nu_rows(p, shift=0):
        return nu[p, 16 + shift:16 + shift + YC]

    def dir_rows(p, shift=0):
        at = p * FR + 8 + shift
        return frame[at:at + YC, :]

    d, n = dir_rows(1), nu_rows(1)
    flux = 0.5 * (nu_rows(0) + n) * (dir_rows(0) - d)
    rr = ri = ii = jnp.zeros((8, 128), F32)

    def fold(value):
        return jnp.sum(value.reshape(YC // 8, 8, 128), axis=0)

    for t in range(ZC):
        p = t + 1
        dz, nz = dir_rows(p + 1), nu_rows(p + 1)
        up, nup = dz, nz
        if p == 2:
            up, nup = jnp.where(start, 0.0, dz), jnp.where(start, 1.0, nz)
        if p == 3:
            flux = jnp.where(start, -0.5 * (1.0 + n) * d, flux)
        ahead = 0.5 * (n + nup) * (d - up)
        flow = ahead - flux
        flow = flow + 0.5 * (n + nu_rows(p, 1)) * (d - dir_rows(p, 1))
        flow = flow + 0.5 * (n + nu_rows(p, -1)) * (d - dir_rows(p, -1))
        nx = jnp.where(last, 1.0, roll(n, -1, 1))
        dx = jnp.where(last, 0.0, roll(d, -1, 1))
        fx = 0.5 * (n + nx) * (d - dx)
        flow = flow + (fx - jnp.where(first, -0.5 * (n + 1.0) * d, roll(fx, 1, 1)))
        value = jnp.where(held, d, flow)
        r = resid[t]
        zdir[t] = d
        image[t] = value
        if t < 2:
            message[t], message[2 + t] = value, r
        rr, ri, ii = rr + fold(r * r), ri + fold(r * value), ii + fold(value * value)
        d, n, flux = dz, nz, ahead

    zdir[ZC], zdir[ZC + 1] = dir_rows(ZC + 1), dir_rows(ZC + 2)
    parts = (rr, ri, ii)
    line = lane_iota((1, 128))
    packed = jnp.zeros((1, 128), F32)
    for k, part in enumerate(parts):
        packed = jnp.where(line == k, jnp.sum(part), packed)
    sums[...] = jnp.broadcast_to(packed[None], sums.shape)


def output_kernel(sums, zdir, image, resid, message, correction, lin_residual, rms):
    total = jnp.sum(sums[...], axis=0)
    beta_sq = total[0:1, 0:1] + 1e-06
    beta = jnp.sqrt(beta_sq)
    h_one = total[0:1, 1:2] / beta_sq
    denom = total[0:1, 2:3] / beta_sq - h_one * h_one * (1e-06 / beta_sq) + 1e-06
    gamma = h_one / denom
    correction[...] = zdir[2:] * gamma[None]
    lin_residual[0:ZC - 2] = resid[2:] - gamma[None] * image[2:]
    lin_residual[ZC - 2:ZC] = message[2:4] - gamma[None] * message[0:2]
    rms[...] = jnp.broadcast_to(beta * (1.0 / np.sqrt(float(NZ * NY * NX))), rms.shape)


def call(kernel, out_shape, scratch=(), **extra):
    return pl.pallas_call(
        kernel,
        out_shape=out_shape,
        scratch_shapes=scratch,
        compiler_params=pltpu.CompilerParams(vmem_limit_bytes=VMEM_LIMIT),
        **extra,
    )


def struct(*shape):
    return jax.ShapeDtypeStruct(shape, F32)


def cyclic(count, step):
    return [(i, (i + step) % count) for i in range(count)]


def shards(iterate, source, region, fixed_mask):
    far = pl.BlockSpec(memory_space=pltpu.HBM)
    cells = (ZC, YC, 128)
    arguments = [
        pltpu.with_memory_space_constraint(argument, pltpu.HBM)
        for argument in (iterate, source, region, fixed_mask)
    ]
    edge = (2, ZC, 8, 128)
    z_one, z_two, up, down = call(
        edge_kernel,
        (struct(160, 128), struct(160, 128), struct(176, 128), struct(176, 128)),
        scratch=[
            pltpu.VMEM(edge, F32), pltpu.VMEM(edge, F32),
            pltpu.VMEM((2, 1, 8, 128), jnp.int32), pltpu.VMEM((2, 1, 8, 128), jnp.int32),
            pltpu.SemaphoreType.DMA((14,)),
        ],
        in_specs=[far] * 4,
    )(*arguments)
    lo = lax.ppermute(up, "gy", cyclic(GY, 1))
    hi = lax.ppermute(down, "gy", cyclic(GY, -1))
    z_one = lax.ppermute(z_one, "gz", cyclic(GZ, 1))
    z_two = lax.ppermute(z_two, "gz", cyclic(GZ, 1))
    kept = (
        struct(GZ, 72, 128), struct(18, WIDE, 128), struct(*cells), struct(24 * FR, 128),
        struct(19, WIDE, 128), struct(18, FR, 128), struct(ZC, FR, 128), struct(2, FR, 128),
    )
    *state, frames = call(
        inner_kernel,
        kept,
        scratch=[
            pltpu.VMEM((1, YC, 128), jnp.int32), pltpu.VMEM((1, YC, 128), jnp.int32),
            pltpu.SemaphoreType.DMA((4,)),
        ],
        in_specs=[far] * 4,
        cost_estimate=COST,
    )(*arguments)
    lo, frames = lax.optimization_barrier((lo, frames))
    corners = call(corner_kernel, struct(56, 128))(lo, hi)
    corners = lax.ppermute(corners, "gz", cyclic(GZ, 1))
    state = call(
        halo_kernel, kept, cost_estimate=COST,
        input_output_aliases={4 + k: k for k in range(len(kept))},
    )(z_one, z_two, lo, hi, *state, frames)
    chunks, nu, resid, *_, frames = call(
        corner_residual_kernel, kept,
        input_output_aliases={1 + k: k for k in range(len(kept))},
    )(corners, *state)
    windows = lax.all_to_all(chunks, "gz", 0, 0, tiled=True)
    sent = call(
        modes_kernel,
        struct(GZ, 40, 128),
        scratch=[
            pltpu.VMEM((NZ, LANES), F32), pltpu.VMEM((NZ + 16, 384), F32),
        ],
    )(windows, *[jnp.asarray(table) for table in tables()])
    returned = lax.all_to_all(sent, "gz", 0, 0, tiled=True)
    zdir, image, message, sums = call(
        image_kernel,
        (
            struct(ZC + 2, YC, 128), struct(*cells), struct(4, YC, 128),
            struct(GZ * GY, 1, 128),
        ),
        scratch=[pltpu.VMEM((19 * FR, 128), F32)],
    )(returned, nu, resid, frames)
    message = lax.ppermute(message, "gz", cyclic(GZ, -1))
    sums = lax.all_to_all(sums, ("gz", "gy"), 0, 0, tiled=True)
    correction, lin_residual, rms = call(
        output_kernel, (struct(*cells), struct(*cells), struct(1, 128))
    )(sums, zdir, image, resid, message)
    return correction, lin_residual, rms[0, 0]


def solution(mesh):
    placed = (P("gz", "gy", None),) * 4
    return jax.shard_map(
        shards,
        mesh=mesh,
        in_specs=placed,
        out_specs=(P("gz", "gy", None), P("gz", "gy", None), P()),
        check_vma=False,
    )
```

```python
import functools

import jax
import jax.numpy as jnp
import ml_dtypes
import numpy as np
from jax import lax
from jax.experimental import pallas as pl
from jax.experimental.pallas import tpu as pltpu
from jax.sharding import PartitionSpec as P

F32 = jnp.float32
BF16 = jnp.bfloat16
NZ, NY, NX = 512, 256, 128
GZ, GY = 32, 4
ZC, YC = NZ // GZ, NY // GY
FR = YC + 16
WIDE = FR + 16
WR, WC, RING = 23, 22, 3
LANES = 512
YP, XP = 4, 8
ROW0 = (0, 17, 33, 49)
VMEM_LIMIT = 40 * 1024 * 1024
COST = pl.CostEstimate(flops=4_000_000, bytes_accessed=8_000_000, transcendentals=0)


def segments(block):
    found = [(WC * (row // 4), row) for row in range(block, WR, 4)]
    if block < 3:
        found = [(0, found[-1][1]), (RING - block, found[0][1])] + found[1:]
    return found


def window_places():
    place = np.full((8, LANES), -1000, np.int32)
    for block in range(4):
        parts = segments(block) + [(128, None)]
        for (begin, row), (end, _) in zip(parts[:-1], parts[1:]):
            for lane in range(begin, end):
                column = (lane - WC * (row // 4)) % 128
                if column < WC:
                    place[0, 128 * block + lane] = row
                    place[1, 128 * block + lane] = column
    return place


def tables():
    index = np.arange(NZ, dtype=np.int64)
    phase = (index[:, None] + 1) * (index[None, :] + 1) % (2 * (NZ + 1))
    table = np.sqrt(2.0 / (NZ + 1)) * np.sin(np.pi * phase / (NZ + 1))
    table = table.astype(np.float32)
    high = table.astype(ml_dtypes.bfloat16)
    low = (table - high.astype(np.float32)).astype(ml_dtypes.bfloat16)
    lam = 2.0 - 2.0 * np.cos(np.pi * (index + 1.0) / (NZ + 1))
    lam = np.broadcast_to(lam.astype(np.float32)[:, None], (NZ, 128))
    there, back = [np.roll(t, 2, 1) for t in (high, low)], [np.roll(t, 2, 0) for t in (high, low)]
    return *there, *back, np.ascontiguousarray(lam), window_places()


def lane_iota(shape):
    return lax.broadcasted_iota(jnp.int32, shape, len(shape) - 1)


def roll(value, shift, axis):
    return pltpu.roll(value, shift % value.shape[axis], axis)


def start_all(pairs, sems):
    copies = [pltpu.make_async_copy(x, y, sems.at[k]) for k, (x, y) in enumerate(pairs)]
    for copy in copies:
        copy.start()
    return copies


def edge_kernel(it, src, reg, msk, z_one, z_two, up, down, e_it, e_src, e_reg, e_msk, sems):
    half = YC // 2
    pairs = [
        (it.at[ZC - 3], z_one.at[0:YC]), (it.at[ZC - 2], z_one.at[YC:2 * YC]),
        (it.at[ZC - 1, 0:half], z_one.at[2 * YC:]), (it.at[ZC - 1, half:], z_two.at[0:half]),
        (src.at[ZC - 2], z_two.at[half:half + YC]), (src.at[ZC - 1], z_two.at[half + YC:]),
    ]
    for side, row in enumerate((0, YC - 8)):
        rows = pl.ds(row, 8)
        pairs += [
            (it.at[:, rows], e_it.at[side]),
            (src.at[:, rows], e_src.at[side]),
            (reg.at[0:1, rows], e_reg.at[side]),
            (msk.at[0:1, rows], e_msk.at[side]),
        ]
    copies = start_all(pairs, sems)
    for copy in copies[6:]:
        copy.wait()
    for z in range(ZC):
        up[5 * z:5 * z + 5] = e_it[1, z, 3:8]
        down[6 * z:6 * z + 6] = e_it[0, z, 0:6]
        up[80 + 4 * z:84 + 4 * z] = e_src[1, z, 4:8]
        down[96 + 4 * z:100 + 4 * z] = e_src[0, z, 0:4]
    up[144:149] = e_reg[1, 0, 3:8].astype(F32)
    up[149:153] = e_msk[1, 0, 4:8].astype(F32)
    up[153:176] = jnp.zeros((23, 128), F32)
    down[160:165] = e_reg[0, 0, 0:5].astype(F32)
    down[165:169] = e_msk[0, 0, 0:4].astype(F32)
    down[169:176] = jnp.zeros((7, 128), F32)
    for copy in copies[:6]:
        copy.wait()


def corner_kernel(lo, hi, out):
    out[0:15] = lo[65:80]
    out[15:33] = hi[78:96]
    out[33:41] = lo[136:144]
    out[41:49] = hi[152:160]
    out[49:56] = jnp.zeros((7, 128), F32)


INNER, OUTER = ((8, YC),), ((0, 16), (YC, 16))


def edge_lanes(count):
    lane = lane_iota((count, 128))
    return lane == 0, lane == 127


def level(frame, p, span, shift=0):
    return frame[p, pl.ds(8 + span[0] + shift, span[1])]


def set_nu(p, span, field, right, nu, iron, last):
    u, uz = level(field, p, span), level(field, p + 1, span)
    if p == 2:
        uz = jnp.where(lax.axis_index("gz") == 0, 0.0, uz)
    ux = jnp.where(last, 0.0, roll(u, -1, 1))
    right[p, pl.ds(*span)] = ux
    dz = uz - u
    dy = level(field, p, span, 1) - u
    dx = ux - u
    bsq = dz * dz + dy * dy + dx * dx
    bsq = bsq * bsq
    nu[p, pl.ds(8 + span[0], span[1])] = jnp.where(iron, 0.05 + bsq / (bsq + 9.0), 1.0)


def set_residuals(span, steps, field, right, nu, drive, flat, rows, resid, first, last):
    start = lax.axis_index("gz") == 0
    begin, count = span
    copper, held = flat[0, pl.ds(*span)] == 1.0, flat[1, pl.ds(*span)] == 1.0
    own = max(begin, 8)
    own = slice(own - begin, min(begin + count, 8 + YC) - begin)
    kept = pl.ds(begin + own.start - 8, own.stop - own.start)
    p = steps[0]
    flux = 0.5 * (level(nu, p, span) + level(nu, p + 1, span)) * (
        level(field, p, span) - level(field, p + 1, span)
    )
    for t in steps:
        p = t + 1
        u, n = level(field, p, span), level(nu, p, span)
        uz, nz = level(field, p + 1, span), level(nu, p + 1, span)
        if p == 2:
            uz, nz = jnp.where(start, 0.0, uz), jnp.where(start, 1.0, nz)
        if p == 3:
            flux = jnp.where(start, -0.5 * (1.0 + n) * u, flux)
        ahead = 0.5 * (n + nz) * (u - uz)
        flow = ahead - flux
        flux = ahead
        flow = flow + 0.5 * (n + level(nu, p, span, 1)) * (u - level(field, p, span, 1))
        flow = flow + 0.5 * (n + level(nu, p, span, -1)) * (u - level(field, p, span, -1))
        nx = jnp.where(last, 1.0, roll(n, -1, 1))
        fx = 0.5 * (n + nx) * (u - right[p, pl.ds(*span)])
        flow = flow + (fx - jnp.where(first, -0.5 * (n + 1.0) * u, roll(fx, 1, 1)))
        value = -jnp.where(held, u, flow - jnp.where(copper, drive[t, pl.ds(*span)], 0.0))
        rows[pl.ds(t * FR + begin, count), :] = value
        resid[t, kept] = value[own]


def set_means(span, rows, first, last):
    begin, count = 16 * FR + span[0], span[1]
    total = rows[pl.ds(begin, count), :]
    rows[pl.ds(begin + FR, count), :] = 2.0 * total + 0.5 * (
        rows[pl.ds(begin - 1, count), :] + rows[pl.ds(begin + 1, count), :]
        + jnp.where(last, float(ZC), roll(total, -1, 1))
        + jnp.where(first, float(ZC), roll(total, 1, 1))
    )


def work(spans, planes, steps, field, right, nu, drive, flat, rows, resid):
    for span in spans:
        first, last = edge_lanes(span[1])
        iron = flat[0, pl.ds(*span)] == 2.0
        for p in planes:
            set_nu(p, span, field, right, nu, iron, last)
    for span in spans:
        first, last = edge_lanes(span[1])
        set_residuals(
            span, steps, field, right, nu, drive, flat, rows, resid, first, last
        )


def sum_planes(spans, nu, rows):
    for span in spans:
        total = level(nu, 1, span)
        for p in range(2, 17):
            total = total + level(nu, p, span)
        rows[pl.ds(16 * FR + span[0], span[1]), :] = total
    for span in spans:
        set_means(span, rows, *edge_lanes(span[1]))


def pack(rows, chunks, parts_y, tiles):
    lane = lane_iota((8, 128))
    places = [(lane - 16 * xp) & 127 for xp in range(XP)]
    for yp in parts_y:
        for block in range(4):
            parts = segments(block)
            turned = {}
            for begin, row in parts:
                at = ROW0[yp] + row + 4
                turned[row] = [
                    roll(
                        rows[pl.ds(8 * tile * FR + at, 8, stride=FR), :],
                        WC * (row // 4) + RING, 1,
                    )
                    for tile in tiles
                ]
            for xp in range(XP):
                values = turned[parts[0][1]]
                for begin, row in parts[1:]:
                    later = places[xp] >= begin
                    values = [jnp.where(later, x, y) for x, y in zip(turned[row], values)]
                peer, at = yp * XP + xp, 16 * block
                for tile, value in zip(tiles, values):
                    if tile < 2:
                        chunks[peer, at + 8 * tile:at + 8 * tile + 8, :] = value
                    else:
                        chunks[peer, 64 + 2 * block:66 + 2 * block, :] = value[0:2]


BEHIND, HERE = range(0, 3), range(3, 18)


def inner_kernel(it, src, reg, msk, chunks, nu, resid, rows, field, right, drive, flat,
                 reg_in, msk_in, sems):
    own = slice(8, 8 + YC)
    copies = start_all(
        (
            (it, field.at[3:19, 16:16 + YC]), (src.at[0:ZC - 2], drive.at[2:ZC, own]),
            (reg.at[0:1], reg_in), (msk.at[0:1], msk_in),
        ),
        sems,
    )
    rows[18 * FR:24 * FR, :] = jnp.zeros((6 * FR, 128), F32)
    for copy in copies:
        copy.wait()
    flat[0, own] = reg_in[0].astype(F32)
    flat[1, own] = msk_in[0].astype(F32)
    work(INNER, HERE, range(3, ZC), field, right, nu, drive, flat, rows, resid)
    pack(rows, chunks, (1, 2), (1,))


def halo_kernel(lo, hi, *refs):
    chunks, nu, resid, rows, field, right, drive, flat = refs[8:]
    column = lax.axis_index("gy")

    def below(value):
        return jnp.where(column == 0, 0.0, value)

    def above(value):
        return jnp.where(column == GY - 1, 0.0, value)

    for z in range(ZC):
        field[z + 3, 11:16] = below(lo[5 * z:5 * z + 5])
        field[z + 3, 80:86] = above(hi[6 * z:6 * z + 6])
    for z in range(ZC - 2):
        drive[z + 2, 4:8] = lo[80 + 4 * z:84 + 4 * z]
        drive[z + 2, 72:76] = hi[96 + 4 * z:100 + 4 * z]
    flat[0, 3:8] = below(lo[144:149])
    flat[0, 72:77] = above(hi[160:165])
    flat[1, 4:8] = lo[149:153]
    flat[1, 72:76] = hi[165:169]
    work(OUTER, HERE, range(3, ZC), field, right, nu, drive, flat, rows, resid)
    pack(rows, chunks, (0, 3), (1,))


def behind_kernel(z_one, z_two, *refs):
    chunks, nu, resid, rows, field, right, drive, flat = refs[8:]
    half = YC // 2
    field[0, 16:16 + YC] = z_one[0:YC]
    field[1, 16:16 + YC] = z_one[YC:2 * YC]
    field[2, 16:16 + half] = z_one[2 * YC:]
    field[2, 16 + half:16 + YC] = z_two[0:half]
    for t in range(2):
        drive[t, 8:8 + YC] = z_two[half + YC * t:half + YC * t + YC]
    work(INNER, BEHIND, range(0, 3), field, right, nu, drive, flat, rows, resid)
    sum_planes(INNER, nu, rows)
    pack(rows, chunks, (1, 2), (0, 2))


def corner_residual_kernel(corners, *refs):
    chunks, nu, resid, rows, field, right, drive, flat = refs[8:]
    column = lax.axis_index("gy")
    for p in range(3):
        field[p, 11:16] = jnp.where(column == 0, 0.0, corners[5 * p:5 * p + 5])
        field[p, 80:86] = jnp.where(column == GY - 1, 0.0, corners[15 + 6 * p:21 + 6 * p])
    for t in range(2):
        drive[t, 4:8] = corners[33 + 4 * t:37 + 4 * t]
        drive[t, 72:76] = corners[41 + 4 * t:45 + 4 * t]
    work(OUTER, BEHIND, range(0, 3), field, right, nu, drive, flat, rows, resid)
    sum_planes(OUTER, nu, rows)
    pack(rows, chunks, (0, 3), (0, 2))


def product(high, low, right_high, right_low):
    left = jnp.concatenate([high, low, high], axis=1)
    right = jnp.concatenate([right_high, right_high, right_low], axis=0)
    return jnp.dot(left, right, preferred_element_type=F32)


def modes_kernel(got, ahead_high, ahead_low, high, low, lam, spots, out, lines, back):
    group, column = lax.axis_index("gz"), lax.axis_index("gy")
    yp, xp = lax.div(group, XP), lax.rem(group, XP)
    s_high, s_low = ahead_high[...], ahead_low[...]
    for half in range(2):
        value = jnp.concatenate(
            [
                got[:, 16 * block:16 * block + 16, :].reshape(NZ, 128)
                for block in (2 * half, 2 * half + 1)
            ],
            axis=1,
        )
        v_high = value.astype(BF16)
        v_low = (value - v_high.astype(F32)).astype(BF16)
        lines[:, 256 * half:256 * half + 256] = product(s_high, s_low, v_high, v_low)

    sums = jnp.sum(got[:, 64:72, :], axis=0) * (1.0 / NZ)
    mean = [sums[2 * b:2 * b + 1] for b in range(4)]
    faces = [sums[2 * b + 1:2 * b + 2] for b in range(4)]
    turned = [pltpu.roll(spots[:, 128 * b:128 * b + 128], 16 * xp, 1) for b in range(4)]
    row = jnp.concatenate([place[0:1] for place in turned], axis=1)
    col = jnp.concatenate([place[1:2] for place in turned], axis=1)
    ypos = column * YC + 16 * yp + jnp.where(yp > 0, 1, 0) + row - 4
    xpos = 16 * xp - RING + col
    inside = (row >= 0) & (xpos >= 0) & (xpos < NX) & (ypos >= 0) & (ypos < NY)
    right = [0.5 * (m + roll(m, -1, 1)) for m in mean]
    left = [roll(r, 1, 1) for r in right]
    above = [0.5 * (mean[b] + mean[b + 1]) for b in range(3)]
    above.append(0.5 * (mean[3] + roll(mean[0], -WC, 1)))
    below = [roll(above[3], WC, 1)] + above[:3]

    spot = lane_iota((LANES, 384))
    own = jnp.where(yp == 0, 1, 0)
    halo = jnp.where(yp == 0, 0, 16)
    inner = (spot - 16 * xp) & 127
    line = RING + jnp.where(spot < 256, own + 8 * (spot >> 7) + (inner >> 4), halo)
    pick = 128 * (line & 3) + ((WC * (line >> 2) + RING + (spot & 15) + 16 * xp) & 127)
    choose = jnp.where(lax.broadcasted_iota(jnp.int32, (LANES, 384), 0) == pick, 1.0, 0.0)
    choose = choose.astype(BF16)
    s_high, s_low = high[...], low[...]
    total = None
    for start in range(0, NZ, 128):
        part = slice(start, start + 128)
        lam_rows = lam[part, :]
        vhat = [lines[part, 128 * b:128 * b + 128] for b in range(4)]
        factor = [
            jnp.where(inside[:, 128 * b:128 * b + 128], 0.6 / (faces[b] + lam_rows * mean[b]), 0.0)
            for b in range(4)
        ]
        w = [factor[b] * vhat[b] for b in range(4)]
        for _ in range(3):
            after = w[1:] + [roll(w[0], -WC, 1)]
            before = [roll(w[3], WC, 1)] + w[:3]
            near = [
                above[b] * after[b] + below[b] * before[b]
                + right[b] * roll(w[b], -1, 1) + left[b] * roll(w[b], 1, 1)
                for b in range(4)
            ]
            w = [0.4 * w[b] + factor[b] * (vhat[b] + near[b]) for b in range(4)]
        w = jnp.concatenate(w, axis=1)
        w_high = w.astype(BF16)
        w_low = (w - w_high.astype(F32)).astype(BF16)
        w_high = jnp.dot(w_high, choose, preferred_element_type=F32).astype(BF16)
        w_low = jnp.dot(w_low, choose, preferred_element_type=F32).astype(BF16)
        term = product(high[:, part], low[:, part], w_high, w_low)
        total = term if total is None else total + term
    back[8:8 + NZ, :] = total
    back[0:8, :] = total[NZ - 8:]
    back[8 + NZ:, :] = total[:8]

    sub = lax.broadcasted_iota(jnp.int32, (8, 128), 0)
    pattern = (((lane_iota((8, 128)) >> 4) + sub - xp) & 7) == 0
    for peer in range(GZ):
        at = 8 + ZC * peer
        for block in range(2):
            lanes = slice(128 * block, 128 * block + 128)
            out[peer, 16 * block:16 * block + 16, :] = back[at:at + ZC, lanes]
            out[peer, 32 + block:33 + block, :] = back[at - 1:at, lanes]
            out[peer, 34 + block:35 + block, :] = back[at + ZC:at + ZC + 1, lanes]
            piece = back[at + 8 * block:at + 8 * block + 8, 256:384]
            piece = jnp.sum(jnp.where(pattern, piece, 0.0), axis=0, keepdims=True)
            out[peer, 36 + block:37 + block, :] = piece
            out[peer, 38 + block:39 + block, :] = back[at + ZC + 1:at + ZC + 2, lanes]


def image_kernel(got, nu, resid, flat, zdir, image, message, sums, frame):
    lane = lane_iota((8, 128))
    places = [(lane >> 4) == k for k in range(8)]

    def spread(tiles, jj):
        value = tiles[0]
        for xp in range(1, XP):
            value = jnp.where(places[(jj + xp) % 8], tiles[xp], value)
        return roll(value, -16 * jj, 1)

    for yp in range(YP):
        for block in range(2):
            for tile in range(2):
                at = 16 * block + 8 * tile
                tiles = [got[yp * XP + xp, at:at + 8, :] for xp in range(XP)]
                for jj in range(8):
                    y = 8 + 16 * yp + 8 * block + jj
                    frame[pl.ds((1 + 8 * tile) * FR + y, 8, stride=FR), :] = spread(tiles, jj)
        tiles = [got[yp * XP + xp, 32:40, :] for xp in range(XP)]
        for jj in range(8):
            value = spread(tiles, jj)
            y = 8 + 16 * yp + jj
            for k in range(2):
                frame[y + 8 * k:y + 8 * k + 1, :] = value[k:k + 1]
                for p, row in ((17, 2), (18, 6)):
                    at = p * FR + y + 8 * k
                    frame[at:at + 1, :] = value[row + k:row + k + 1]

    sub = lax.broadcasted_iota(jnp.int32, (8, 128), 0)
    turn = ((lane >> 4) + sub) & 7
    for yp, y in ((0, 7), (YP - 1, 8 + YC)):
        for tile in range(2):
            value = jnp.zeros((8, 128), F32)
            for xp in range(XP):
                line = got[yp * XP + xp, 36 + tile:37 + tile, :]
                value = jnp.where(turn == xp, jnp.broadcast_to(line, (8, 128)), value)
            value = pltpu.roll(value, 0, 1, stride=16, stride_axis=0)
            frame[pl.ds((1 + 8 * tile) * FR + y, 8, stride=FR), :] = value

    lane = lane_iota((YC, 128))
    first, last = lane == 0, lane == 127
    held = flat[1, 8:8 + YC] == 1.0

    start = lax.axis_index("gz") == 0

    def nu_rows(p, shift=0):
        return nu[p, 16 + shift:16 + shift + YC]

    def dir_rows(p, shift=0):
        at = p * FR + 8 + shift
        return frame[at:at + YC, :]

    d, n = dir_rows(1), nu_rows(1)
    flux = 0.5 * (nu_rows(0) + n) * (dir_rows(0) - d)
    rr = ri = ii = jnp.zeros((8, 128), F32)

    def fold(value):
        return jnp.sum(value.reshape(YC // 8, 8, 128), axis=0)

    for t in range(ZC):
        p = t + 1
        dz, nz = dir_rows(p + 1), nu_rows(p + 1)
        up, nup = dz, nz
        if p == 2:
            up, nup = jnp.where(start, 0.0, dz), jnp.where(start, 1.0, nz)
        if p == 3:
            flux = jnp.where(start, -0.5 * (1.0 + n) * d, flux)
        ahead = 0.5 * (n + nup) * (d - up)
        flow = ahead - flux
        flow = flow + 0.5 * (n + nu_rows(p, 1)) * (d - dir_rows(p, 1))
        flow = flow + 0.5 * (n + nu_rows(p, -1)) * (d - dir_rows(p, -1))
        nx = jnp.where(last, 1.0, roll(n, -1, 1))
        dx = jnp.where(last, 0.0, roll(d, -1, 1))
        fx = 0.5 * (n + nx) * (d - dx)
        flow = flow + (fx - jnp.where(first, -0.5 * (n + 1.0) * d, roll(fx, 1, 1)))
        value = jnp.where(held, d, flow)
        r = resid[t]
        zdir[t] = d
        image[t] = value
        if t < 2:
            message[t], message[2 + t] = value, r
        rr, ri, ii = rr + fold(r * r), ri + fold(r * value), ii + fold(value * value)
        d, n, flux = dz, nz, ahead

    zdir[ZC], zdir[ZC + 1] = dir_rows(ZC + 1), dir_rows(ZC + 2)
    parts = (rr, ri, ii)
    line = lane_iota((1, 128))
    packed = jnp.zeros((1, 128), F32)
    for k, part in enumerate(parts):
        packed = jnp.where(line == k, jnp.sum(part), packed)
    sums[...] = jnp.broadcast_to(packed[None], sums.shape)


def output_kernel(sums, zdir, image, resid, message, correction, lin_residual, rms):
    total = jnp.sum(sums[...], axis=0)
    beta_sq = total[0:1, 0:1] + 1e-06
    beta = jnp.sqrt(beta_sq)
    h_one = total[0:1, 1:2] / beta_sq
    denom = total[0:1, 2:3] / beta_sq - h_one * h_one * (1e-06 / beta_sq) + 1e-06
    gamma = h_one / denom
    correction[...] = zdir[2:] * gamma[None]
    lin_residual[0:ZC - 2] = resid[2:] - gamma[None] * image[2:]
    lin_residual[ZC - 2:ZC] = message[2:4] - gamma[None] * message[0:2]
    rms[...] = jnp.broadcast_to(beta * (1.0 / np.sqrt(float(NZ * NY * NX))), rms.shape)


def call(kernel, out_shape, scratch=(), **extra):
    return pl.pallas_call(
        kernel,
        out_shape=out_shape,
        scratch_shapes=scratch,
        compiler_params=pltpu.CompilerParams(vmem_limit_bytes=VMEM_LIMIT),
        **extra,
    )


def struct(*shape):
    return jax.ShapeDtypeStruct(shape, F32)


def cyclic(count, step):
    return [(i, (i + step) % count) for i in range(count)]


def shards(iterate, source, region, fixed_mask):
    far = pl.BlockSpec(memory_space=pltpu.HBM)
    cells = (ZC, YC, 128)
    arguments = [
        pltpu.with_memory_space_constraint(argument, pltpu.HBM)
        for argument in (iterate, source, region, fixed_mask)
    ]
    edge = (2, ZC, 8, 128)
    z_one, z_two, up, down = call(
        edge_kernel,
        (struct(160, 128), struct(160, 128), struct(176, 128), struct(176, 128)),
        scratch=[
            pltpu.VMEM(edge, F32), pltpu.VMEM(edge, F32),
            pltpu.VMEM((2, 1, 8, 128), jnp.int32), pltpu.VMEM((2, 1, 8, 128), jnp.int32),
            pltpu.SemaphoreType.DMA((14,)),
        ],
        in_specs=[far] * 4,
    )(*arguments)
    lo = lax.ppermute(up, "gy", cyclic(GY, 1))
    hi = lax.ppermute(down, "gy", cyclic(GY, -1))
    z_one = lax.ppermute(z_one, "gz", cyclic(GZ, 1))
    z_two = lax.ppermute(z_two, "gz", cyclic(GZ, 1))
    kept = (
        struct(GZ, 72, 128), struct(18, WIDE, 128), struct(*cells), struct(24 * FR, 128),
        struct(19, WIDE, 128), struct(18, FR, 128), struct(ZC, FR, 128), struct(2, FR, 128),
    )
    *state, frames = call(
        inner_kernel,
        kept,
        scratch=[
            pltpu.VMEM((1, YC, 128), jnp.int32), pltpu.VMEM((1, YC, 128), jnp.int32),
            pltpu.SemaphoreType.DMA((4,)),
        ],
        in_specs=[far] * 4,
        cost_estimate=COST,
    )(*arguments)
    lo, frames = lax.optimization_barrier((lo, frames))
    corners = call(corner_kernel, struct(56, 128))(lo, hi)
    corners = lax.ppermute(corners, "gz", cyclic(GZ, 1))
    state = call(
        halo_kernel, kept, cost_estimate=COST,
        input_output_aliases={2 + k: k for k in range(len(kept))},
    )(lo, hi, *state, frames)
    state = call(
        behind_kernel, kept, cost_estimate=COST,
        input_output_aliases={2 + k: k for k in range(len(kept))},
    )(z_one, z_two, *state)
    chunks, nu, resid, *_, frames = call(
        corner_residual_kernel, kept,
        input_output_aliases={1 + k: k for k in range(len(kept))},
    )(corners, *state)
    windows = lax.all_to_all(chunks, "gz", 0, 0, tiled=True)
    sent = call(
        modes_kernel,
        struct(GZ, 40, 128),
        scratch=[
            pltpu.VMEM((NZ, LANES), F32), pltpu.VMEM((NZ + 16, 384), F32),
        ],
    )(windows, *[jnp.asarray(table) for table in tables()])
    returned = lax.all_to_all(sent, "gz", 0, 0, tiled=True)
    zdir, image, message, sums = call(
        image_kernel,
        (
            struct(ZC + 2, YC, 128), struct(*cells), struct(4, YC, 128),
            struct(GZ * GY, 1, 128),
        ),
        scratch=[pltpu.VMEM((19 * FR, 128), F32)],
    )(returned, nu, resid, frames)
    message = lax.ppermute(message, "gz", cyclic(GZ, -1))
    sums = lax.all_to_all(sums, ("gz", "gy"), 0, 0, tiled=True)
    correction, lin_residual, rms = call(
        output_kernel, (struct(*cells), struct(*cells), struct(1, 128))
    )(sums, zdir, image, resid, message)
    return correction, lin_residual, rms[0, 0]


def solution(mesh):
    placed = (P("gz", "gy", None),) * 4
    return jax.shard_map(
        shards,
        mesh=mesh,
        in_specs=placed,
        out_specs=(P("gz", "gy", None), P("gz", "gy", None), P()),
        check_vma=False,
    )
```
